32 devices in a mesh: face: 4 (over x, core), tile: 8 (over z, y).
Axes of the slice: x: 2, y: 2, z: 4, core: 2. Of those that a mesh axis runs over, the one named last changes fastest.
Arguments:
- predicted_field: bfloat16 [16, 2048, 128], P(None, ('face', 'tile')), may hold values from -6 to 6
- parent_band_holder: int32 [2048, 2], P(('face', 'tile')), may hold values from 0 to 31, all different within a row; in each aligned block of 64 rows (0 to 63, 64 to 127, ...) at most 8 rows name the same one
- parent_band_slot: int32 [2048, 2], P(('face', 'tile')), may hold values from 0 to 63
- neighbour_positions: int32 [4, 2048, 128], P(None, ('face', 'tile')), may hold values from 0 to 255
- unscaled_neighbour_factor: float32 [4, 2048, 128], P(None, ('face', 'tile')), may hold values from 0.05 to 1
- truth_field: float32 [256, 1024], P('tile', 'face'), may hold values from -6 to 6
Outputs:
- predicted_field_slope: float32 [16, 2048, 128], P(None, ('face', 'tile'))
The draws below stay inside these ranges and needn't reach their ends.
Inputs may be any that keep to these rules, and one draw needn't show every extreme that they name: `parent_band_holder`: the two entries of a row differ. Within the 64 rows of one device no device is named more than 8 times, and some device is named exactly 8 times.
All inputs are finite; a program needn't handle non-finite values.
Results may differ from the reference program's by a relative error of at most 0.0003.
Values may be sent and summed in bfloat16 or wider, within the bound.
A program may use at most 128 MiB of HBM per device.

```python
import math
import jax
import jax.numpy as jnp
import numpy as np
from jax import lax

PARTICIPANT_NUM = 16
PIXELS_PER_BAND = 128
BLK_DEV = 64
RANGE = 8
J = 4
SLOT = 8
LAT_DEV = 32
BAND_COUNT_ALL = 2048
NLAT = 256
NLON = 1024
N_FACE = 4
N_TILE = 8


def touch_ends(result, own_key, low, largest):
    longest = result.shape.index(max(result.shape))
    spots = []
    for shift in (0, 1):
        where = [jax.random.randint(jax.random.fold_in(own_key, axis), (), 0, length) for axis, length in enumerate(result.shape)]
        where[longest] = (where[longest] + shift) % result.shape[longest]
        spots.append(tuple(where))
    return result.at[spots[0]].set(low).at[spots[1]].set(largest)


def steps_of(stream_key, dims, pieces, low, top_value):
    def one(axis_at, blocks):
        steps = jax.random.uniform(jax.random.fold_in(jax.random.fold_in(stream_key, 6), axis_at), (blocks,), jnp.float32, low / len(pieces), top_value / len(pieces))
        return jnp.repeat(jnp.exp(steps), dims[axis_at] // blocks).reshape((-1,) + (1,) * (len(dims) - axis_at - 1))

    loudness = one(*pieces[0])
    for cut in pieces[1:]:
        loudness = loudness * one(*cut)
    return loudness


def assign_block(own_key, own, number, rows, number_of, top, limit, slope):
    order = jax.random.permutation(own_key, number_of)
    heavy_load, ordinary = shares(number_of, rows * top, limit, slope, True), shares(number_of, rows * top, limit, slope, False)
    places = jnp.arange(number_of)

    def named(sizes, rotation):
        used = int((sizes > 0).sum())
        fixed = max(1, used // 4)
        passed = fixed + (places - fixed + rotation * (used - fixed)) % max(1, number_of - fixed)
        return jnp.zeros((number_of,), jnp.int32).at[order[jnp.where(places < fixed, places, passed)]].set(jnp.asarray(sizes, jnp.int32))

    sizes = jnp.where(number % 4 == 0, named(heavy_load, number // 4), named(ordinary, number - number // 4 - 1))
    mixed = jax.random.permutation(jax.random.fold_in(own, 3), number_of)
    giver, taker = mixed[0:number_of // 2 * 2:2], mixed[1:number_of // 2 * 2:2]
    room = jnp.minimum(sizes[giver] - 1, limit - sizes[taker]) // 2
    room = jnp.where((giver == order[0]) | (taker == order[0]) | (sizes[taker] == 0), 0, jnp.maximum(room, 0))
    passed = jax.random.randint(jax.random.fold_in(own, 4), (number_of // 2,), 0, 1 << 20) % (room + 1)
    sizes = sizes.at[giver].add(-passed).at[taker].add(passed)
    members = jnp.searchsorted(jnp.cumsum(sizes), jnp.arange(rows * top), side="right").astype(jnp.int32)
    table = members.reshape(top, rows).T
    table = table[jax.random.permutation(jax.random.fold_in(own, 1), rows)]
    rotation = jax.random.randint(jax.random.fold_in(own, 2), (rows, 1), 0, top)
    return jnp.take_along_axis(table, (jnp.arange(top)[None, :] + rotation) % top, axis=1)


def shares(amount, total, limit, slope, full):
    portions = [(1 << 20) // math.isqrt(rank ** slope) + 1 for rank in range(1, amount + 1)]
    largest = limit if full else min(limit, max(-(-total // amount), total * portions[0] // sum(portions)))
    least = 1 if total - largest >= amount - 1 else 0
    counts, spare = [largest] + [least] * (amount - 1), total - largest - least * (amount - 1)
    while spare > 0:
        movable = [i for i in range(1, amount) if counts[i] < largest] or [i for i in range(1, amount) if counts[i] < limit]
        pool, budget = sum([portions[i] for i in movable]), spare
        for i in movable:
            extra = min(limit - counts[i], max(1, budget * portions[i] // pool), spare)
            counts[i] = counts[i] + extra
            spare = spare - extra
    return np.array(counts)


def normal_values(stream_key, extent, width, limit, split=(), held_as=jnp.bfloat16):
    values = width * jax.random.normal(stream_key, extent, jnp.float32)
    if split:
        values = values * steps_of(stream_key, extent, split, -0.22, 0.18)
    return jnp.clip(values, -limit, limit).astype(held_as)


def setup_inputs(seed: int = 0) -> dict:
    seeds = jax.random.split(jax.random.key(seed), 7)
    predicted_field = normal_values(seeds[0], (PARTICIPANT_NUM, BAND_COUNT_ALL, PIXELS_PER_BAND), 1.0, 6.0, ((1, 32),))
    parent_band_holder_keys = jax.random.split(jax.random.fold_in(seeds[1], 1), BAND_COUNT_ALL // BLK_DEV)
    parent_band_holder_turns = jax.random.permutation(jax.random.fold_in(seeds[1], 3), BAND_COUNT_ALL // BLK_DEV)
    parent_band_holder = jax.vmap(lambda own, number: assign_block(jax.random.fold_in(seeds[1], 2), own, number, BLK_DEV, N_FACE * N_TILE, 2, SLOT, 1))(parent_band_holder_keys, parent_band_holder_turns).reshape((BAND_COUNT_ALL, 2))
    parent_band_slot = touch_ends(jax.random.randint(seeds[2], (BAND_COUNT_ALL, 2), 0, BLK_DEV), jax.random.fold_in(seeds[2], 1), 0, BLK_DEV - 1).astype(jnp.int32)
    neighbour_positions = touch_ends(jax.random.randint(seeds[3], (J, BAND_COUNT_ALL, PIXELS_PER_BAND), 0, 2 * PIXELS_PER_BAND), jax.random.fold_in(seeds[3], 1), 0, (2 * PIXELS_PER_BAND) - 1).astype(jnp.int32)
    unscaled_neighbour_factor = jnp.clip(0.05 + 0.95 * jax.random.uniform(seeds[4], (J, BAND_COUNT_ALL, PIXELS_PER_BAND), jnp.float32) ** steps_of(seeds[4], (J, BAND_COUNT_ALL, PIXELS_PER_BAND), ((1, 32),), -0.2, 0.2), 0.05, 1.0)
    truth_field = normal_values(seeds[5], (NLAT, NLON), 1.0, 6.0, ((0, 8), (1, 4)), jnp.float32)
    return dict(predicted_field=predicted_field, parent_band_holder=parent_band_holder, parent_band_slot=parent_band_slot, neighbour_positions=neighbour_positions, unscaled_neighbour_factor=unscaled_neighbour_factor, truth_field=truth_field)


FLOOR = 0.01

def pair_push(first, second, weight, participant_count):
    diff = first[:participant_count] - second[:participant_count]
    square_sum = diff * diff + FLOOR
    inverse_power = square_sum ** (-0.75)
    spread = lax.optimization_barrier(jnp.mean(square_sum * inverse_power, axis=0))
    observed = first[participant_count] - second[participant_count]
    mismatch = (observed * observed + FLOOR) ** 0.25 - spread
    return weight / participant_count * mismatch * diff * inverse_power

def gather_weighted(values, neighbour_positions, norm_weight):
    participant_count = values.shape[0]
    band_ids = jnp.arange(values.shape[1], dtype=jnp.int32)[:, None]
    summed = jnp.zeros((participant_count,) + neighbour_positions.shape[1:], jnp.float32)
    for point in range(neighbour_positions.shape[0]):
        picked = values[:, band_ids, neighbour_positions[point]]
        summed = summed + picked.astype(jnp.float32) * norm_weight[point][None]
    return summed

def reference(predicted_field, parent_band_holder, parent_band_slot, neighbour_positions, unscaled_neighbour_factor, truth_field):
    participant_count = predicted_field.shape[0]
    parent_band = (parent_band_holder * BLK_DEV + parent_band_slot).reshape(-1).astype(jnp.int32)
    incoming_bands = jnp.take(predicted_field, parent_band, axis=1).reshape(participant_count, BAND_COUNT_ALL, 2 * PIXELS_PER_BAND)
    norm_weight = unscaled_neighbour_factor / lax.optimization_barrier(jnp.sum(unscaled_neighbour_factor, axis=0, keepdims=True))
    regridded = gather_weighted(incoming_bands, neighbour_positions, norm_weight)
    field = regridded.reshape(participant_count, N_FACE, N_TILE, LAT_DEV, 2 * PIXELS_PER_BAND)
    field = field.transpose(0, 2, 3, 1, 4).reshape(participant_count, NLAT, NLON)
    stacked = jnp.concatenate([field, truth_field[None]], axis=0)
    gradient = jnp.zeros((participant_count, NLAT, NLON), jnp.float32)
    for offset in range(1, RANGE + 1):
        pushed = pair_push(stacked[:, :-offset], stacked[:, offset:], 1.0 / offset, participant_count)
        zero_rows = jnp.zeros((participant_count, offset, NLON), jnp.float32)
        gradient = gradient - jnp.concatenate([pushed, zero_rows], axis=1)
        gradient = gradient + jnp.concatenate([zero_rows, pushed], axis=1)
    for offset in range(1, RANGE + 1):
        pushed = pair_push(stacked, jnp.roll(stacked, -offset, axis=2), 1.0 / offset, participant_count)
        gradient = gradient - pushed + jnp.roll(pushed, offset, axis=2)
    grad_blocks = gradient.reshape(participant_count, N_TILE, LAT_DEV, N_FACE, 2 * PIXELS_PER_BAND)
    grad_blocks = grad_blocks.transpose(0, 3, 1, 2, 4).reshape(participant_count, BAND_COUNT_ALL, PIXELS_PER_BAND)
    unused, pullback = jax.vjp(lambda values: gather_weighted(values, neighbour_positions, norm_weight), jnp.zeros((participant_count, BAND_COUNT_ALL, 2 * PIXELS_PER_BAND), jnp.float32))
    incoming_slope_parts = pullback(grad_blocks)[0].reshape(participant_count, 2 * BAND_COUNT_ALL, PIXELS_PER_BAND)
    predicted_field_slope = jnp.zeros((participant_count, BAND_COUNT_ALL, PIXELS_PER_BAND), jnp.float32).at[:, parent_band].add(incoming_slope_parts)
    return predicted_field_slope
```

```python
import functools

import jax
import jax.numpy as jnp
from jax import lax
from jax.experimental import pallas as pl
from jax.experimental.pallas import tpu as pltpu
from jax.sharding import PartitionSpec as P

RANGE = 8
FLOOR = 0.01
LANES = 128
VMEM = pltpu.VMEM
SMEM = pltpu.SMEM


def spec(space):
    return pl.BlockSpec(memory_space=space)


def root_of(diff):
    return lax.rsqrt(lax.rsqrt(diff * diff + FLOOR))


def lane_pick(values, index):
    return jnp.take_along_axis(values, index, axis=1, mode="promise_in_bounds")


def lane_ids():
    return lax.broadcasted_iota(jnp.int32, (16, LANES), 1)


def regrid_kernel(place, incoming, positions, factors, field, heads, tails, weights):
    total = factors[0] + factors[1] + factors[2] + factors[3]
    for j in range(4):
        weights[j] = factors[j] / total
    members = field.shape[1]
    lane = lax.broadcasted_iota(jnp.int32, (members, LANES), 1)
    per_tile = LANES // RANGE
    for group in range(heads.shape[0]):
        def row_step(r, carry):
            head, tail = carry
            row = group * per_tile + r
            for half in range(2):
                g = 2 * row + half
                first = incoming[place[2 * g]].astype(jnp.float32)
                second = incoming[place[2 * g + 1]].astype(jnp.float32)
                summed = None
                for j in range(4):
                    at = jnp.broadcast_to(positions[j, pl.ds(g, 1), :], (members, LANES))
                    low = at & (LANES - 1)
                    picked = jnp.where(at < LANES, lane_pick(first, low), lane_pick(second, low))
                    term = picked * weights[j, pl.ds(g, 1), :]
                    summed = term if summed is None else summed + term
                field[g] = summed
                mine = (lane >> 3) == r
                if half == 0:
                    head = jnp.where(mine, pltpu.roll(summed, r * RANGE, 1), head)
                else:
                    tail = jnp.where(mine, pltpu.roll(summed, r * RANGE + RANGE, 1), tail)
            return head, tail

        zero = jnp.zeros((members, LANES), jnp.float32)
        head, tail = lax.fori_loop(0, per_tile, row_step, (zero, zero), unroll=2)
        heads[group] = head
        tails[group] = tail


def push_of(first, second, observed_root, scale):
    diff = first - second
    square = diff * diff + FLOOR
    inverse = lax.rsqrt(square)
    root = lax.rsqrt(inverse)
    spread = jnp.sum(root, axis=0, keepdims=True) * (1.0 / first.shape[0])
    mismatch = (observed_root - spread) * scale
    return mismatch * (diff * (root * inverse * inverse))


def score_kernel(
    edge, place, field, above, below, heads, tails, left_tails, right_heads,
    root_tall, root_wide, root_left, root_right, positions, factors,
    slots, ext, grad, weights,
):
    bands, members = field.shape[0], field.shape[1]
    rows = bands // 2
    halo = 2 * RANGE
    total = factors[0] + factors[1] + factors[2] + factors[3]
    for j in range(4):
        weights[j] = factors[j] / total
    ext[pl.ds(0, halo)] = above[...]
    ext[pl.ds(halo, bands)] = field[...]
    ext[pl.ds(halo + bands, halo)] = below[...]
    grad[...] = jnp.zeros_like(grad)

    def tall_step(a, carry):
        for half in range(2):
            mine = ext[2 * a + half]
            own = jnp.zeros_like(mine)
            for k in range(1, RANGE + 1):
                inside = (a >= edge[0]) & (a + k < edge[1])
                scale = jnp.where(inside, 1.0 / (k * members), 0.0)
                other = 2 * (a + k) + half
                push = push_of(
                    mine, ext[other],
                    root_tall[2 * k - 2 + half, pl.ds(a, 1), :], scale,
                )
                own = own - push
                grad[other] = grad[other] + push
            grad[2 * a + half] = grad[2 * a + half] + own
        return carry

    lax.fori_loop(0, rows + RANGE, tall_step, 0)

    lane = lax.broadcasted_iota(jnp.int32, (members, LANES), 1)

    sub = lane & (RANGE - 1)
    per_tile = LANES // RANGE
    for group in range(heads.shape[0]):
        head, tail = heads[group], tails[group]
        left, right = left_tails[group], right_heads[group]
        head_grad = jnp.zeros_like(head)
        tail_grad = jnp.zeros_like(tail)
        for k in range(1, RANGE + 1):
            crossing = sub >= RANGE - k
            scale = 1.0 / (k * members)
            shift = RANGE - k
            moved = pltpu.roll(head, shift, 1) if shift else head
            push = push_of(left, moved, root_left[k - 1, pl.ds(group, 1), :], scale)
            push = jnp.where(crossing, push, 0.0)
            back = pltpu.roll(push, LANES - shift, 1) if shift else push
            head_grad = head_grad + back
            moved = pltpu.roll(right, shift, 1) if shift else right
            push = push_of(tail, moved, root_right[k - 1, pl.ds(group, 1), :], scale)
            tail_grad = tail_grad - jnp.where(crossing, push, 0.0)

        def spread_step(r, carry):
            g = halo + 2 * (group * per_tile + r)
            back = pltpu.roll(head_grad, LANES - r * RANGE, 1)
            grad[g] = grad[g] + jnp.where(lane < RANGE, back, 0.0)
            back = pltpu.roll(tail_grad, LANES - RANGE - r * RANGE, 1)
            grad[g + 1] = grad[g + 1] + jnp.where(lane >= LANES - RANGE, back, 0.0)
            return carry

        lax.fori_loop(0, per_tile, spread_step, 0)

    def wide_step(r, carry):
        g = 2 * r
        west, east = field[g], field[g + 1]
        west_grad, east_grad = grad[halo + g], grad[halo + g + 1]
        for k in range(1, RANGE + 1):
            scale = 1.0 / (k * members)
            within = lane < LANES - k
            after = lane >= k
            west_next = pltpu.roll(west, LANES - k, 1)
            east_next = pltpu.roll(east, LANES - k, 1)
            west_push = push_of(
                west, jnp.where(within, west_next, east_next),
                root_wide[2 * k - 2, pl.ds(r, 1), :], scale,
            )
            east_push = push_of(
                east, east_next, root_wide[2 * k - 1, pl.ds(r, 1), :], scale
            )
            east_push = jnp.where(within, east_push, 0.0)
            west_back = pltpu.roll(west_push, k, 1)
            east_back = pltpu.roll(east_push, k, 1)
            west_grad = west_grad - west_push + jnp.where(after, west_back, 0.0)
            east_grad = east_grad - east_push + jnp.where(after, east_back, west_back)
        for half, value in ((0, west_grad), (1, east_grad)):
            adjoint(g + half, value)
        return carry

    spots = lax.broadcasted_iota(jnp.int32, (2 * LANES, LANES), 0)
    contract = (((1,), (1,)), ((), ()))

    def adjoint(g, value):
        matrix = jnp.zeros((2 * LANES, LANES), jnp.float32)
        for j in range(4):
            at = positions[j, pl.ds(g, 1), :]
            matrix = matrix + jnp.where(spots == at, weights[j, pl.ds(g, 1), :], 0.0)
        high = matrix.astype(jnp.bfloat16)
        low = (matrix - high.astype(jnp.float32)).astype(jnp.bfloat16)
        value_high = value.astype(jnp.bfloat16)
        value_low = (value - value_high.astype(jnp.float32)).astype(jnp.bfloat16)
        slope = (
            lax.dot_general(value_high, high, contract, preferred_element_type=jnp.float32)
            + lax.dot_general(value_low, high, contract, preferred_element_type=jnp.float32)
            + lax.dot_general(value_high, low, contract, preferred_element_type=jnp.float32)
        )
        slots[place[2 * g]] = slope[:, :LANES]
        slots[place[2 * g + 1]] = slope[:, LANES:]

    lax.fori_loop(0, rows, wide_step, 0)


def collect_kernel(wanted, returned, slope, summed):
    bands = slope.shape[1]
    summed[...] = jnp.zeros_like(summed)

    def step(i, carry):
        at = wanted[i]
        summed[at] = summed[at] + returned[i]
        return carry

    lax.fori_loop(0, returned.shape[0], step, 0, unroll=8)
    for g in range(bands):
        slope[:, g, :] = summed[g]


def halves(planes):
    return jnp.stack([p[:, at : at + LANES] for p in planes for at in (0, LANES)])


def shifted(cells, axis, step, closed):
    count = lax.axis_size(axis)
    ends = count if closed else count - 1
    pairs = [(i, (i + 1) % count) for i in range(ends)]
    if step < 0:
        pairs = [(b, a) for a, b in pairs]
    return lax.ppermute(cells, axis, pairs)


def local(
    predicted_field,
    parent_band_holder,
    parent_band_slot,
    neighbour_positions,
    unscaled_neighbour_factor,
    truth_field,
):
    members, bands, pixels = predicted_field.shape
    tile_count = lax.axis_size("tile")
    device_count = lax.axis_size(("face", "tile"))
    slot_count = max(2, 4 * bands // device_count)
    slots_all = device_count * slot_count
    rows, cols = bands // 2, 2 * pixels
    groups = rows * RANGE // LANES

    owner = parent_band_holder.reshape(-1)
    order = jnp.arange(2 * bands, dtype=jnp.int32)
    before = (owner[:, None] == owner[None, :]) & (order[None, :] < order[:, None])
    place = owner * slot_count + jnp.sum(before.astype(jnp.int32), axis=1)
    held = place[None, :] == jnp.arange(slots_all, dtype=jnp.int32)[:, None]
    wanted = bands + jnp.sum(
        jnp.where(held, parent_band_slot.reshape(-1)[None, :] - bands, 0), axis=1
    )
    asked = lax.all_to_all(
        wanted.reshape(device_count, slot_count), ("face", "tile"),
        split_axis=0, concat_axis=0, tiled=True,
    ).reshape(-1)
    strips = jnp.transpose(predicted_field, (1, 0, 2))
    outgoing = jnp.take(strips, jnp.minimum(asked, bands - 1), axis=0)
    incoming = lax.all_to_all(
        outgoing, ("face", "tile"), split_axis=0, concat_axis=0, tiled=True
    )

    truth_above = shifted(truth_field[rows - RANGE :], "tile", 1, False)
    truth_below = shifted(truth_field[:RANGE], "tile", -1, False)
    truth_tall = jnp.concatenate([truth_above, truth_field, truth_below], axis=0)
    root_tall = halves(
        [root_of(truth_tall[: rows + RANGE] - truth_tall[k : k + rows + RANGE]) for k in range(1, RANGE + 1)]
    )
    root_wide = halves(
        [root_of(truth_field - jnp.roll(truth_field, -k, axis=1)) for k in range(1, RANGE + 1)]
    )
    truth_heads = truth_field[:, :RANGE].reshape(groups, LANES)
    truth_tails = truth_field[:, cols - RANGE :].reshape(groups, LANES)
    truth_left = shifted(truth_tails, "face", 1, True)
    truth_right = shifted(truth_heads, "face", -1, True)
    root_left = jnp.stack(
        [root_of(truth_left - jnp.roll(truth_heads, RANGE - k, axis=1)) for k in range(1, RANGE + 1)]
    )
    root_right = jnp.stack(
        [root_of(truth_tails - jnp.roll(truth_right, RANGE - k, axis=1)) for k in range(1, RANGE + 1)]
    )

    f32 = jnp.float32
    side = jax.ShapeDtypeStruct((groups, members, LANES), f32)
    field, heads, tails = pl.pallas_call(
        regrid_kernel,
        out_shape=(jax.ShapeDtypeStruct((bands, members, pixels), f32), side, side),
        in_specs=[spec(SMEM), spec(VMEM), spec(VMEM), spec(VMEM)],
        out_specs=(spec(VMEM), spec(VMEM), spec(VMEM)),
        scratch_shapes=[pltpu.VMEM((4, bands, pixels), f32)],
        compiler_params=pltpu.CompilerParams(vmem_limit_bytes=32 << 20),
        name="regrid",
    )(place, incoming, neighbour_positions, unscaled_neighbour_factor)

    halo = 2 * RANGE
    above = shifted(field[bands - halo :], "tile", 1, False)
    below = shifted(field[:halo], "tile", -1, False)
    left_tails = shifted(tails, "face", 1, True)
    right_heads = shifted(heads, "face", -1, True)
    tile = lax.axis_index("tile")
    edge = jnp.stack(
        [RANGE - tile * rows, RANGE + (tile_count - tile) * rows]
    ).astype(jnp.int32)

    slots = pl.pallas_call(
        score_kernel,
        out_shape=jax.ShapeDtypeStruct((slots_all, members, pixels), f32),
        in_specs=[spec(SMEM), spec(SMEM)] + [spec(VMEM)] * 13,
        out_specs=spec(VMEM),
        scratch_shapes=[
            pltpu.VMEM((bands + 2 * halo, members, pixels), f32),
            pltpu.VMEM((bands + 2 * halo, members, pixels), f32),
            pltpu.VMEM((4, bands, pixels), f32),
        ],
        compiler_params=pltpu.CompilerParams(vmem_limit_bytes=32 << 20),
        name="score",
    )(
        edge, place, field, above, below, heads, tails, left_tails, right_heads,
        root_tall, root_wide, root_left, root_right,
        neighbour_positions, unscaled_neighbour_factor,
    )
    returned = lax.all_to_all(
        slots, ("face", "tile"), split_axis=0, concat_axis=0, tiled=True
    )
    return pl.pallas_call(
        collect_kernel,
        out_shape=jax.ShapeDtypeStruct((members, bands, pixels), f32),
        in_specs=[spec(SMEM), spec(VMEM)],
        out_specs=spec(VMEM),
        scratch_shapes=[pltpu.VMEM((bands + 8, members, pixels), f32)],
        compiler_params=pltpu.CompilerParams(vmem_limit_bytes=32 << 20),
        name="collect",
    )(asked, returned)


def solution(mesh):
    in_specs = (
        P(None, ("face", "tile"), None),
        P(("face", "tile"), None),
        P(("face", "tile"), None),
        P(None, ("face", "tile"), None),
        P(None, ("face", "tile"), None),
        P("tile", "face"),
    )
    out_specs = P(None, ("face", "tile"), None)
    return jax.shard_map(local, mesh=mesh, in_specs=in_specs, out_specs=out_specs, check_vma=False)
```

```python
import functools

import jax
import jax.numpy as jnp
from jax import lax
from jax.experimental import pallas as pl
from jax.experimental.pallas import tpu as pltpu
from jax.sharding import PartitionSpec as P

RANGE = 8
FLOOR = 0.01
LANES = 128
STEPS = 32000.0
SHARE = 16384.0
VMEM = pltpu.VMEM
SMEM = pltpu.SMEM


def spec(space):
    return pl.BlockSpec(memory_space=space)


def root_of(diff):
    return lax.rsqrt(lax.rsqrt(diff * diff + FLOOR))


def lane_pick(values, index):
    return jnp.take_along_axis(values, index, axis=1, mode="promise_in_bounds")


def lane_ids():
    return lax.broadcasted_iota(jnp.int32, (16, LANES), 1)


def regrid_kernel(place, incoming, positions, factors, field, heads, tails, weights):
    total = factors[0] + factors[1] + factors[2] + factors[3]
    for j in range(4):
        weights[j] = factors[j] / total
    members = field.shape[1]
    lane = lax.broadcasted_iota(jnp.int32, (members, LANES), 1)
    per_tile = LANES // RANGE
    for group in range(heads.shape[0]):
        def row_step(r, carry):
            head, tail = carry
            row = group * per_tile + r
            for half in range(2):
                g = 2 * row + half
                first = incoming[place[2 * g]].astype(jnp.float32)
                second = incoming[place[2 * g + 1]].astype(jnp.float32)
                summed = None
                for j in range(4):
                    at = jnp.broadcast_to(positions[j, pl.ds(g, 1), :], (members, LANES))
                    low = at & (LANES - 1)
                    picked = jnp.where(at < LANES, lane_pick(first, low), lane_pick(second, low))
                    term = picked * weights[j, pl.ds(g, 1), :]
                    summed = term if summed is None else summed + term
                field[g] = summed
                mine = (lane >> 3) == r
                if half == 0:
                    head = jnp.where(mine, pltpu.roll(summed, r * RANGE, 1), head)
                else:
                    tail = jnp.where(mine, pltpu.roll(summed, r * RANGE + RANGE, 1), tail)
            return head, tail

        zero = jnp.zeros((members, LANES), jnp.float32)
        head, tail = lax.fori_loop(0, per_tile, row_step, (zero, zero), unroll=2)
        heads[group] = head
        tails[group] = tail


def push_of(first, second, observed_root, scale):
    diff = first - second
    square = diff * diff + FLOOR
    inverse = lax.rsqrt(square)
    root = lax.rsqrt(inverse)
    spread = jnp.sum(root, axis=0, keepdims=True) * (1.0 / first.shape[0])
    mismatch = (observed_root - spread) * scale
    return mismatch * (diff * (root * inverse * inverse))


def prepare_kernel(
    truth, above, below, heads, tails, left, right, positions, factors,
    root_tall, root_wide, root_left, root_right, high, low, tall, weights,
):
    rows = truth.shape[0]
    tall[pl.ds(0, RANGE)] = above[...]
    tall[pl.ds(RANGE, rows)] = truth[...]
    tall[pl.ds(RANGE + rows, RANGE)] = below[...]
    span = rows + RANGE
    for k in range(1, RANGE + 1):
        root = root_of(tall[pl.ds(0, span), :] - tall[pl.ds(k, span), :])
        root_tall[2 * k - 2] = root[:, :LANES]
        root_tall[2 * k - 1] = root[:, LANES:]
        west, east = truth[:, :LANES], truth[:, LANES:]
        lane = lax.broadcasted_iota(jnp.int32, west.shape, 1)
        west_next = pltpu.roll(west, LANES - k, 1)
        east_next = pltpu.roll(east, LANES - k, 1)
        root_wide[2 * k - 2] = root_of(west - jnp.where(lane < LANES - k, west_next, east_next))
        root_wide[2 * k - 1] = root_of(east - east_next)
        shift = RANGE - k
        near = heads[...]
        far = right[...]
        if shift:
            near = jnp.concatenate([near[:, LANES - shift :], near[:, : LANES - shift]], axis=1)
            far = jnp.concatenate([far[:, LANES - shift :], far[:, : LANES - shift]], axis=1)
        root_left[k - 1] = root_of(left[...] - near)
        root_right[k - 1] = root_of(tails[...] - far)
    total = factors[0] + factors[1] + factors[2] + factors[3]
    for j in range(4):
        weights[j] = factors[j] / total
    spots = lax.broadcasted_iota(jnp.int32, (2 * LANES, LANES), 0)

    def step(g, carry):
        matrix = jnp.zeros((2 * LANES, LANES), jnp.float32)
        for j in range(4):
            at = positions[j, pl.ds(g, 1), :]
            matrix = matrix + jnp.where(spots == at, weights[j, pl.ds(g, 1), :], 0.0)
        matrix = matrix.T
        top = matrix.astype(jnp.bfloat16)
        high[g] = top
        low[g] = (matrix - top.astype(jnp.float32)).astype(jnp.bfloat16)
        return carry

    lax.fori_loop(0, high.shape[0], step, 0)


def score_kernel(
    edge, place, field, above, below, heads, tails, left_tails, right_heads,
    root_tall, root_wide, root_left, root_right, high_far, low_far,
    slots, ext, grad, scales, high, low, arrived,
):
    bands, members = field.shape[0], field.shape[1]
    rows = bands // 2
    halo = 2 * RANGE
    fetch_high = pltpu.make_async_copy(high_far, high, arrived.at[0])
    fetch_low = pltpu.make_async_copy(low_far, low, arrived.at[1])
    fetch_high.start()
    fetch_low.start()
    ext[pl.ds(0, halo)] = above[...]
    ext[pl.ds(halo, bands)] = field[...]
    ext[pl.ds(halo + bands, halo)] = below[...]
    grad[...] = jnp.zeros_like(grad)

    def tall_step(a, carry):
        for half in range(2):
            mine = ext[2 * a + half]
            own = jnp.zeros_like(mine)
            for k in range(1, RANGE + 1):
                inside = (a >= edge[0]) & (a + k < edge[1])
                scale = jnp.where(inside, 1.0 / (k * members), 0.0)
                other = 2 * (a + k) + half
                push = push_of(
                    mine, ext[other],
                    root_tall[2 * k - 2 + half, pl.ds(a, 1), :], scale,
                )
                own = own - push
                grad[other] = grad[other] + push
            grad[2 * a + half] = grad[2 * a + half] + own
        return carry

    lax.fori_loop(0, rows + RANGE, tall_step, 0)

    lane = lax.broadcasted_iota(jnp.int32, (members, LANES), 1)

    sub = lane & (RANGE - 1)
    per_tile = LANES // RANGE
    for group in range(heads.shape[0]):
        head, tail = heads[group], tails[group]
        left, right = left_tails[group], right_heads[group]
        head_grad = jnp.zeros_like(head)
        tail_grad = jnp.zeros_like(tail)
        for k in range(1, RANGE + 1):
            crossing = sub >= RANGE - k
            scale = 1.0 / (k * members)
            shift = RANGE - k
            moved = pltpu.roll(head, shift, 1) if shift else head
            push = push_of(left, moved, root_left[k - 1, pl.ds(group, 1), :], scale)
            push = jnp.where(crossing, push, 0.0)
            back = pltpu.roll(push, LANES - shift, 1) if shift else push
            head_grad = head_grad + back
            moved = pltpu.roll(right, shift, 1) if shift else right
            push = push_of(tail, moved, root_right[k - 1, pl.ds(group, 1), :], scale)
            tail_grad = tail_grad - jnp.where(crossing, push, 0.0)

        def spread_step(r, carry):
            g = halo + 2 * (group * per_tile + r)
            back = pltpu.roll(head_grad, LANES - r * RANGE, 1)
            grad[g] = grad[g] + jnp.where(lane < RANGE, back, 0.0)
            back = pltpu.roll(tail_grad, LANES - RANGE - r * RANGE, 1)
            grad[g + 1] = grad[g + 1] + jnp.where(lane >= LANES - RANGE, back, 0.0)
            return carry

        lax.fori_loop(0, per_tile, spread_step, 0)

    def wide_step(r, carry):
        g = 2 * r
        west, east = field[g], field[g + 1]
        west_grad, east_grad = grad[halo + g], grad[halo + g + 1]
        for k in range(1, RANGE + 1):
            scale = 1.0 / (k * members)
            within = lane < LANES - k
            after = lane >= k
            west_next = pltpu.roll(west, LANES - k, 1)
            east_next = pltpu.roll(east, LANES - k, 1)
            west_push = push_of(
                west, jnp.where(within, west_next, east_next),
                root_wide[2 * k - 2, pl.ds(r, 1), :], scale,
            )
            east_push = push_of(
                east, east_next, root_wide[2 * k - 1, pl.ds(r, 1), :], scale
            )
            east_push = jnp.where(within, east_push, 0.0)
            west_back = pltpu.roll(west_push, k, 1)
            east_back = pltpu.roll(east_push, k, 1)
            west_grad = west_grad - west_push + jnp.where(after, west_back, 0.0)
            east_grad = east_grad - east_push + jnp.where(after, east_back, west_back)
        for half, value in ((0, west_grad), (1, east_grad)):
            adjoint(g + half, value)
        return carry

    slot_count = slots.shape[1] - 1

    def adjoint(g, value):
        value_high = value.astype(jnp.bfloat16)
        value_low = (value - value_high.astype(jnp.float32)).astype(jnp.bfloat16)
        both = jnp.concatenate([value_high, value_low], axis=0)
        main = jnp.dot(both, high[g], preferred_element_type=jnp.float32)
        slope = (
            main[:members] + main[members:]
            + jnp.dot(value_high, low[g], preferred_element_type=jnp.float32)
        )
        for half in range(2):
            part = slope[:, half * LANES : (half + 1) * LANES]
            largest = jnp.max(jnp.abs(part), axis=1, keepdims=True)
            step = jnp.maximum(largest, 1e-30) * (1.0 / STEPS)
            code = jnp.round(part * (1.0 / step)).astype(jnp.int32)
            at = place[2 * g + half]
            holder = at // slot_count
            rank = at - holder * slot_count
            slots[holder, rank] = code.astype(jnp.int16)
            power = jnp.ceil(jnp.log2(step))
            share = jnp.round(step * jnp.exp2(-power) * SHARE)
            old = scales[holder]
            old = jnp.where(lane == rank, power.astype(jnp.int32), old)
            scales[holder] = jnp.where(lane == rank + LANES // 2, share.astype(jnp.int32), old)

    fetch_high.wait()
    fetch_low.wait()
    lax.fori_loop(0, rows, wide_step, 0)
    for holder in range(slots.shape[0]):
        slots[holder, slot_count] = scales[holder].astype(jnp.int16)


def collect_kernel(wanted, returned, slope, summed):
    bands = slope.shape[1]
    summed[...] = jnp.zeros_like(summed)

    slot_count = returned.shape[1] - 1

    def step(d, carry):
        scale = returned[d, slot_count].astype(jnp.int32).astype(jnp.float32)
        share = pltpu.roll(scale, LANES // 2, 1) * (1.0 / SHARE)
        step_of = share * jnp.exp2(scale)
        for k in range(slot_count):
            at = wanted[d * slot_count + k]
            code = returned[d, k].astype(jnp.int32).astype(jnp.float32)
            summed[at] = summed[at] + code * step_of[:, k : k + 1]
        return carry

    lax.fori_loop(0, returned.shape[0], step, 0)
    for g in range(bands):
        slope[:, g, :] = summed[g]


def halves(planes):
    return jnp.stack([p[:, at : at + LANES] for p in planes for at in (0, LANES)])


def shifted(cells, axis, step, closed):
    count = lax.axis_size(axis)
    ends = count if closed else count - 1
    pairs = [(i, (i + 1) % count) for i in range(ends)]
    if step < 0:
        pairs = [(b, a) for a, b in pairs]
    return lax.ppermute(cells, axis, pairs)


def local(
    predicted_field,
    parent_band_holder,
    parent_band_slot,
    neighbour_positions,
    unscaled_neighbour_factor,
    truth_field,
):
    members, bands, pixels = predicted_field.shape
    tile_count = lax.axis_size("tile")
    device_count = lax.axis_size(("face", "tile"))
    slot_count = max(2, 4 * bands // device_count)
    slots_all = device_count * slot_count
    rows, cols = bands // 2, 2 * pixels
    groups = rows * RANGE // LANES

    owner = parent_band_holder.reshape(-1)
    order = jnp.arange(2 * bands, dtype=jnp.int32)
    before = (owner[:, None] == owner[None, :]) & (order[None, :] < order[:, None])
    place = owner * slot_count + jnp.sum(before.astype(jnp.int32), axis=1)
    held = place[None, :] == jnp.arange(slots_all, dtype=jnp.int32)[:, None]
    wanted = bands + jnp.sum(
        jnp.where(held, parent_band_slot.reshape(-1)[None, :] - bands, 0), axis=1
    )
    asked = lax.all_to_all(
        wanted.reshape(device_count, slot_count), ("face", "tile"),
        split_axis=0, concat_axis=0, tiled=True,
    ).reshape(-1)
    strips = jnp.transpose(predicted_field, (1, 0, 2))
    outgoing = jnp.take(strips, jnp.minimum(asked, bands - 1), axis=0)
    incoming = lax.all_to_all(
        outgoing, ("face", "tile"), split_axis=0, concat_axis=0, tiled=True
    )

    truth_field, asked_late = lax.optimization_barrier((truth_field, asked))
    truth_above = shifted(truth_field[rows - RANGE :], "tile", 1, False)
    truth_below = shifted(truth_field[:RANGE], "tile", -1, False)
    truth_heads = truth_field[:, :RANGE].reshape(groups, LANES)
    truth_tails = truth_field[:, cols - RANGE :].reshape(groups, LANES)
    truth_left = shifted(truth_tails, "face", 1, True)
    truth_right = shifted(truth_heads, "face", -1, True)
    f32 = jnp.float32
    matrices = jax.ShapeDtypeStruct((bands, pixels, 2 * pixels), jnp.bfloat16)
    root_tall, root_wide, root_left, root_right, high, low = pl.pallas_call(
        prepare_kernel,
        out_shape=(
            jax.ShapeDtypeStruct((2 * RANGE, rows + RANGE, LANES), f32),
            jax.ShapeDtypeStruct((2 * RANGE, rows, LANES), f32),
            jax.ShapeDtypeStruct((RANGE, groups, LANES), f32),
            jax.ShapeDtypeStruct((RANGE, groups, LANES), f32),
            matrices,
            matrices,
        ),
        in_specs=[spec(VMEM)] * 9,
        out_specs=(spec(VMEM),) * 6,
        scratch_shapes=[
            pltpu.VMEM((rows + 2 * RANGE, cols), f32),
            pltpu.VMEM((4, bands, pixels), f32),
        ],
        compiler_params=pltpu.CompilerParams(vmem_limit_bytes=40 << 20),
        cost_estimate=pl.CostEstimate(flops=10**9, bytes_accessed=16 << 20, transcendentals=0),
        name="prepare",
    )(
        truth_field, truth_above, truth_below, truth_heads, truth_tails, truth_left, truth_right,
        neighbour_positions, unscaled_neighbour_factor,
    )

    side = jax.ShapeDtypeStruct((groups, members, LANES), f32)
    field, heads, tails = pl.pallas_call(
        regrid_kernel,
        out_shape=(jax.ShapeDtypeStruct((bands, members, pixels), f32), side, side),
        in_specs=[spec(SMEM), spec(VMEM), spec(VMEM), spec(VMEM)],
        out_specs=(spec(VMEM), spec(VMEM), spec(VMEM)),
        scratch_shapes=[pltpu.VMEM((4, bands, pixels), f32)],
        compiler_params=pltpu.CompilerParams(vmem_limit_bytes=32 << 20),
        name="regrid",
    )(place, incoming, neighbour_positions, unscaled_neighbour_factor)

    halo = 2 * RANGE
    above = shifted(field[bands - halo :], "tile", 1, False)
    below = shifted(field[:halo], "tile", -1, False)
    left_tails = shifted(tails, "face", 1, True)
    right_heads = shifted(heads, "face", -1, True)
    tile = lax.axis_index("tile")
    edge = jnp.stack(
        [RANGE - tile * rows, RANGE + (tile_count - tile) * rows]
    ).astype(jnp.int32)

    slots = pl.pallas_call(
        score_kernel,
        out_shape=jax.ShapeDtypeStruct((device_count, slot_count + 1, members, pixels), jnp.int16),
        in_specs=[spec(SMEM), spec(SMEM)] + [spec(VMEM)] * 11 + [spec(pl.ANY)] * 2,
        out_specs=spec(VMEM),
        scratch_shapes=[
            pltpu.VMEM((bands + 2 * halo, members, pixels), f32),
            pltpu.VMEM((bands + 2 * halo, members, pixels), f32),
            pltpu.VMEM((device_count, members, pixels), jnp.int32),
            pltpu.VMEM((bands, pixels, 2 * pixels), jnp.bfloat16),
            pltpu.VMEM((bands, pixels, 2 * pixels), jnp.bfloat16),
            pltpu.SemaphoreType.DMA((2,)),
        ],
        compiler_params=pltpu.CompilerParams(vmem_limit_bytes=40 << 20),
        name="score",
    )(
        edge, place, field, above, below, heads, tails, left_tails, right_heads,
        root_tall, root_wide, root_left, root_right, high, low,
    )
    returned = lax.all_to_all(
        slots, ("face", "tile"), split_axis=0, concat_axis=0, tiled=True
    )
    return pl.pallas_call(
        collect_kernel,
        out_shape=jax.ShapeDtypeStruct((members, bands, pixels), f32),
        in_specs=[spec(SMEM), spec(VMEM)],
        out_specs=spec(VMEM),
        scratch_shapes=[pltpu.VMEM((bands + 8, members, pixels), f32)],
        compiler_params=pltpu.CompilerParams(vmem_limit_bytes=32 << 20),
        name="collect",
    )(asked, returned)


def solution(mesh):
    in_specs = (
        P(None, ("face", "tile"), None),
        P(("face", "tile"), None),
        P(("face", "tile"), None),
        P(None, ("face", "tile"), None),
        P(None, ("face", "tile"), None),
        P("tile", "face"),
    )
    out_specs = P(None, ("face", "tile"), None)
    return jax.shard_map(local, mesh=mesh, in_specs=in_specs, out_specs=out_specs, check_vma=False)
```

```python
import functools

import jax
import jax.numpy as jnp
from jax import lax
from jax.experimental import pallas as pl
from jax.experimental.pallas import tpu as pltpu
from jax.sharding import PartitionSpec as P

RANGE = 8
FLOOR = 0.01
LANES = 128
STEPS = 32000.0
SHARE = 16384.0
VMEM = pltpu.VMEM
SMEM = pltpu.SMEM


def spec(space):
    return pl.BlockSpec(memory_space=space)


def root_of(diff):
    return lax.rsqrt(lax.rsqrt(diff * diff + FLOOR))


def lane_pick(values, index):
    return jnp.take_along_axis(values, index, axis=1, mode="promise_in_bounds")


def lane_ids():
    return lax.broadcasted_iota(jnp.int32, (16, LANES), 1)


def place_of(number, tiles):
    return (number // tiles, number % tiles)


def greet(count, tiles, me):
    barrier = pltpu.get_barrier_semaphore()

    def step(s, carry):
        other = (me + s) % count
        pl.semaphore_signal(
            barrier, inc=1, device_id=place_of(other, tiles), device_id_type=pl.DeviceIdType.MESH
        )
        return carry

    lax.fori_loop(1, count, step, 0)
    pl.semaphore_wait(barrier, count - 1)


def remote(source, target, sent, arrived, other, tiles):
    return pltpu.make_async_remote_copy(
        src_ref=source, dst_ref=target, send_sem=sent, recv_sem=arrived,
        device_id=place_of(other, tiles), device_id_type=pl.DeviceIdType.MESH,
    )


def fetch_kernel(
    count, tiles, wanted, strips, incoming, asked,
    asked_rows, numbers, outgoing, list_sent, list_got, strip_sent, strip_got, local_sem,
):
    me = lax.axis_index("face") * tiles + lax.axis_index("tile")
    slot_count = outgoing.shape[1]
    bands = strips.shape[0]
    greet(count, tiles, me)

    def ask(s, carry):
        other = (me + s) % count
        remote(wanted.at[other], asked_rows.at[me], list_sent.at[s], list_got.at[s], other, tiles).start()
        return carry

    def heard(s, carry):
        other = (me + s) % count
        remote(wanted.at[other], asked_rows.at[me], list_sent.at[s], list_got.at[s], other, tiles).wait()
        return carry

    lax.fori_loop(1, count, ask, 0)
    asked_rows[me] = wanted[me]
    lax.fori_loop(1, count, heard, 0)
    listing = pltpu.make_async_copy(asked_rows, numbers, local_sem)
    listing.start()
    asked[...] = asked_rows[...]
    listing.wait()

    for k in range(slot_count):
        incoming[me, k] = strips[jnp.minimum(numbers[me, 0, k], bands - 1)]

    def send(s, carry):
        other = (me + s) % count
        for k in range(slot_count):
            outgoing[s, k] = strips[jnp.minimum(numbers[other, 0, k], bands - 1)]
        remote(outgoing.at[s], incoming.at[me], strip_sent.at[s], strip_got.at[s], other, tiles).start()
        return carry

    def got(s, carry):
        other = (me + s) % count
        remote(outgoing.at[s], incoming.at[me], strip_sent.at[s], strip_got.at[s], other, tiles).wait()
        return carry

    lax.fori_loop(1, count, send, 0)
    lax.fori_loop(1, count, got, 0)


def regrid_kernel(place, incoming, positions, factors, field, heads, tails, weights):
    total = factors[0] + factors[1] + factors[2] + factors[3]
    for j in range(4):
        weights[j] = factors[j] / total
    members = field.shape[1]
    lane = lax.broadcasted_iota(jnp.int32, (members, LANES), 1)
    per_tile = LANES // RANGE
    for group in range(heads.shape[0]):
        def row_step(r, carry):
            head, tail = carry
            row = group * per_tile + r
            for half in range(2):
                g = 2 * row + half
                first = incoming[place[2 * g]].astype(jnp.float32)
                second = incoming[place[2 * g + 1]].astype(jnp.float32)
                summed = None
                for j in range(4):
                    at = jnp.broadcast_to(positions[j, pl.ds(g, 1), :], (members, LANES))
                    low = at & (LANES - 1)
                    picked = jnp.where(at < LANES, lane_pick(first, low), lane_pick(second, low))
                    term = picked * weights[j, pl.ds(g, 1), :]
                    summed = term if summed is None else summed + term
                field[g] = summed
                mine = (lane >> 3) == r
                if half == 0:
                    head = jnp.where(mine, pltpu.roll(summed, r * RANGE, 1), head)
                else:
                    tail = jnp.where(mine, pltpu.roll(summed, r * RANGE + RANGE, 1), tail)
            return head, tail

        zero = jnp.zeros((members, LANES), jnp.float32)
        head, tail = lax.fori_loop(0, per_tile, row_step, (zero, zero), unroll=2)
        heads[group] = head
        tails[group] = tail


def push_of(first, second, observed_root, scale):
    diff = first - second
    square = diff * diff + FLOOR
    inverse = lax.rsqrt(square)
    root = lax.rsqrt(inverse)
    spread = jnp.sum(root, axis=0, keepdims=True) * (1.0 / first.shape[0])
    mismatch = (observed_root - spread) * scale
    return mismatch * (diff * (root * inverse * inverse))


def prepare_kernel(
    truth, above, below, heads, tails, left, right, positions, factors,
    root_tall, root_wide, root_left, root_right, high, low, tall, weights,
):
    rows = truth.shape[0]
    tall[pl.ds(0, RANGE)] = above[...]
    tall[pl.ds(RANGE, rows)] = truth[...]
    tall[pl.ds(RANGE + rows, RANGE)] = below[...]
    span = rows + RANGE
    for k in range(1, RANGE + 1):
        root = root_of(tall[pl.ds(0, span), :] - tall[pl.ds(k, span), :])
        root_tall[2 * k - 2] = root[:, :LANES]
        root_tall[2 * k - 1] = root[:, LANES:]
        west, east = truth[:, :LANES], truth[:, LANES:]
        lane = lax.broadcasted_iota(jnp.int32, west.shape, 1)
        west_next = pltpu.roll(west, LANES - k, 1)
        east_next = pltpu.roll(east, LANES - k, 1)
        root_wide[2 * k - 2] = root_of(west - jnp.where(lane < LANES - k, west_next, east_next))
        root_wide[2 * k - 1] = root_of(east - east_next)
        shift = RANGE - k
        near = heads[...]
        far = right[...]
        if shift:
            near = jnp.concatenate([near[:, LANES - shift :], near[:, : LANES - shift]], axis=1)
            far = jnp.concatenate([far[:, LANES - shift :], far[:, : LANES - shift]], axis=1)
        root_left[k - 1] = root_of(left[...] - near)
        root_right[k - 1] = root_of(tails[...] - far)
    total = factors[0] + factors[1] + factors[2] + factors[3]
    for j in range(4):
        weights[j] = factors[j] / total
    spots = lax.broadcasted_iota(jnp.int32, (2 * LANES, LANES), 0)

    def step(g, carry):
        matrix = jnp.zeros((2 * LANES, LANES), jnp.float32)
        for j in range(4):
            at = positions[j, pl.ds(g, 1), :]
            matrix = matrix + jnp.where(spots == at, weights[j, pl.ds(g, 1), :], 0.0)
        matrix = matrix.T
        top = matrix.astype(jnp.bfloat16)
        high[g] = top
        low[g] = (matrix - top.astype(jnp.float32)).astype(jnp.bfloat16)
        return carry

    lax.fori_loop(0, high.shape[0], step, 0)


def score_kernel(
    edge, place, field, above, below, heads, tails, left_tails, right_heads,
    root_tall, root_wide, root_left, root_right, high_far, low_far,
    slots, ext, grad, scales, high, low, arrived,
):
    bands, members = field.shape[0], field.shape[1]
    rows = bands // 2
    halo = 2 * RANGE
    fetch_high = pltpu.make_async_copy(high_far, high, arrived.at[0])
    fetch_low = pltpu.make_async_copy(low_far, low, arrived.at[1])
    fetch_high.start()
    fetch_low.start()
    ext[pl.ds(0, halo)] = above[...]
    ext[pl.ds(halo, bands)] = field[...]
    ext[pl.ds(halo + bands, halo)] = below[...]
    grad[...] = jnp.zeros_like(grad)

    def tall_step(a, carry):
        for half in range(2):
            mine = ext[2 * a + half]
            own = jnp.zeros_like(mine)
            for k in range(1, RANGE + 1):
                inside = (a >= edge[0]) & (a + k < edge[1])
                scale = jnp.where(inside, 1.0 / (k * members), 0.0)
                other = 2 * (a + k) + half
                push = push_of(
                    mine, ext[other],
                    root_tall[2 * k - 2 + half, pl.ds(a, 1), :], scale,
                )
                own = own - push
                grad[other] = grad[other] + push
            grad[2 * a + half] = grad[2 * a + half] + own
        return carry

    lax.fori_loop(0, rows + RANGE, tall_step, 0)

    lane = lax.broadcasted_iota(jnp.int32, (members, LANES), 1)

    sub = lane & (RANGE - 1)
    per_tile = LANES // RANGE
    for group in range(heads.shape[0]):
        head, tail = heads[group], tails[group]
        left, right = left_tails[group], right_heads[group]
        head_grad = jnp.zeros_like(head)
        tail_grad = jnp.zeros_like(tail)
        for k in range(1, RANGE + 1):
            crossing = sub >= RANGE - k
            scale = 1.0 / (k * members)
            shift = RANGE - k
            moved = pltpu.roll(head, shift, 1) if shift else head
            push = push_of(left, moved, root_left[k - 1, pl.ds(group, 1), :], scale)
            push = jnp.where(crossing, push, 0.0)
            back = pltpu.roll(push, LANES - shift, 1) if shift else push
            head_grad = head_grad + back
            moved = pltpu.roll(right, shift, 1) if shift else right
            push = push_of(tail, moved, root_right[k - 1, pl.ds(group, 1), :], scale)
            tail_grad = tail_grad - jnp.where(crossing, push, 0.0)

        def spread_step(r, carry):
            g = halo + 2 * (group * per_tile + r)
            back = pltpu.roll(head_grad, LANES - r * RANGE, 1)
            grad[g] = grad[g] + jnp.where(lane < RANGE, back, 0.0)
            back = pltpu.roll(tail_grad, LANES - RANGE - r * RANGE, 1)
            grad[g + 1] = grad[g + 1] + jnp.where(lane >= LANES - RANGE, back, 0.0)
            return carry

        lax.fori_loop(0, per_tile, spread_step, 0)

    def wide_step(r, carry):
        g = 2 * r
        west, east = field[g], field[g + 1]
        west_grad, east_grad = grad[halo + g], grad[halo + g + 1]
        for k in range(1, RANGE + 1):
            scale = 1.0 / (k * members)
            within = lane < LANES - k
            after = lane >= k
            west_next = pltpu.roll(west, LANES - k, 1)
            east_next = pltpu.roll(east, LANES - k, 1)
            west_push = push_of(
                west, jnp.where(within, west_next, east_next),
                root_wide[2 * k - 2, pl.ds(r, 1), :], scale,
            )
            east_push = push_of(
                east, east_next, root_wide[2 * k - 1, pl.ds(r, 1), :], scale
            )
            east_push = jnp.where(within, east_push, 0.0)
            west_back = pltpu.roll(west_push, k, 1)
            east_back = pltpu.roll(east_push, k, 1)
            west_grad = west_grad - west_push + jnp.where(after, west_back, 0.0)
            east_grad = east_grad - east_push + jnp.where(after, east_back, west_back)
        for half, value in ((0, west_grad), (1, east_grad)):
            adjoint(g + half, value)
        return carry

    slot_count = slots.shape[1] - 1

    def adjoint(g, value):
        value_high = value.astype(jnp.bfloat16)
        value_low = (value - value_high.astype(jnp.float32)).astype(jnp.bfloat16)
        both = jnp.concatenate([value_high, value_low], axis=0)
        main = jnp.dot(both, high[g], preferred_element_type=jnp.float32)
        slope = (
            main[:members] + main[members:]
            + jnp.dot(value_high, low[g], preferred_element_type=jnp.float32)
        )
        for half in range(2):
            part = slope[:, half * LANES : (half + 1) * LANES]
            largest = jnp.max(jnp.abs(part), axis=1, keepdims=True)
            step = jnp.maximum(largest, 1e-30) * (1.0 / STEPS)
            code = jnp.round(part * (1.0 / step)).astype(jnp.int32)
            at = place[2 * g + half]
            holder = at // slot_count
            rank = at - holder * slot_count
            slots[holder, rank] = code.astype(jnp.int16)
            power = jnp.ceil(jnp.log2(step))
            share = jnp.round(step * jnp.exp2(-power) * SHARE)
            old = scales[holder]
            old = jnp.where(lane == rank, power.astype(jnp.int32), old)
            scales[holder] = jnp.where(lane == rank + LANES // 2, share.astype(jnp.int32), old)

    fetch_high.wait()
    fetch_low.wait()
    lax.fori_loop(0, rows, wide_step, 0)
    for holder in range(slots.shape[0]):
        slots[holder, slot_count] = scales[holder].astype(jnp.int16)


def collect_kernel(wanted, returned, slope, summed):
    bands = slope.shape[1]
    summed[...] = jnp.zeros_like(summed)

    slot_count = returned.shape[1] - 1

    def step(d, carry):
        scale = returned[d, slot_count].astype(jnp.int32).astype(jnp.float32)
        share = pltpu.roll(scale, LANES // 2, 1) * (1.0 / SHARE)
        step_of = share * jnp.exp2(scale)
        for k in range(slot_count):
            at = wanted[d * slot_count + k]
            code = returned[d, k].astype(jnp.int32).astype(jnp.float32)
            summed[at] = summed[at] + code * step_of[:, k : k + 1]
        return carry

    lax.fori_loop(0, returned.shape[0], step, 0, unroll=4)
    for g in range(bands):
        slope[:, g, :] = summed[g]


def halves(planes):
    return jnp.stack([p[:, at : at + LANES] for p in planes for at in (0, LANES)])


def shifted(cells, axis, step, closed):
    count = lax.axis_size(axis)
    ends = count if closed else count - 1
    pairs = [(i, (i + 1) % count) for i in range(ends)]
    if step < 0:
        pairs = [(b, a) for a, b in pairs]
    return lax.ppermute(cells, axis, pairs)


def local(
    predicted_field,
    parent_band_holder,
    parent_band_slot,
    neighbour_positions,
    unscaled_neighbour_factor,
    truth_field,
):
    members, bands, pixels = predicted_field.shape
    tile_count = lax.axis_size("tile")
    device_count = lax.axis_size(("face", "tile"))
    slot_count = max(2, 4 * bands // device_count)
    slots_all = device_count * slot_count
    rows, cols = bands // 2, 2 * pixels
    groups = rows * RANGE // LANES

    owner = parent_band_holder.reshape(-1)
    order = jnp.arange(2 * bands, dtype=jnp.int32)
    before = (owner[:, None] == owner[None, :]) & (order[None, :] < order[:, None])
    place = owner * slot_count + jnp.sum(before.astype(jnp.int32), axis=1)
    held = place[None, :] == jnp.arange(slots_all, dtype=jnp.int32)[:, None]
    wanted = bands + jnp.sum(
        jnp.where(held, parent_band_slot.reshape(-1)[None, :] - bands, 0), axis=1
    )
    strips = jnp.transpose(predicted_field, (1, 0, 2))
    lists = jnp.pad(
        wanted.reshape(device_count, 1, slot_count), ((0, 0), (0, 0), (0, LANES - slot_count))
    )
    incoming, asked = pl.pallas_call(
        functools.partial(fetch_kernel, device_count, tile_count),
        out_shape=(
            jax.ShapeDtypeStruct((device_count, slot_count, members, pixels), predicted_field.dtype),
            jax.ShapeDtypeStruct((device_count, 1, LANES), jnp.int32),
        ),
        in_specs=[spec(VMEM), spec(VMEM)],
        out_specs=(spec(VMEM), spec(VMEM)),
        scratch_shapes=[
            pltpu.VMEM((device_count, 1, LANES), jnp.int32),
            pltpu.SMEM((device_count, 1, LANES), jnp.int32),
            pltpu.VMEM((device_count, slot_count, members, pixels), predicted_field.dtype),
            pltpu.SemaphoreType.DMA((device_count,)),
            pltpu.SemaphoreType.DMA((device_count,)),
            pltpu.SemaphoreType.DMA((device_count,)),
            pltpu.SemaphoreType.DMA((device_count,)),
            pltpu.SemaphoreType.DMA,
        ],
        compiler_params=pltpu.CompilerParams(
            collective_id=1, has_side_effects=True, vmem_limit_bytes=24 << 20
        ),
        name="fetch",
    )(lists, strips)
    incoming = incoming.reshape(slots_all, members, pixels)
    asked = asked[:, 0, :slot_count].reshape(-1)

    truth_field, asked_late = lax.optimization_barrier((truth_field, asked))
    truth_above = shifted(truth_field[rows - RANGE :], "tile", 1, False)
    truth_below = shifted(truth_field[:RANGE], "tile", -1, False)
    truth_heads = truth_field[:, :RANGE].reshape(groups, LANES)
    truth_tails = truth_field[:, cols - RANGE :].reshape(groups, LANES)
    truth_left = shifted(truth_tails, "face", 1, True)
    truth_right = shifted(truth_heads, "face", -1, True)
    f32 = jnp.float32
    matrices = jax.ShapeDtypeStruct((bands, pixels, 2 * pixels), jnp.bfloat16)
    root_tall, root_wide, root_left, root_right, high, low = pl.pallas_call(
        prepare_kernel,
        out_shape=(
            jax.ShapeDtypeStruct((2 * RANGE, rows + RANGE, LANES), f32),
            jax.ShapeDtypeStruct((2 * RANGE, rows, LANES), f32),
            jax.ShapeDtypeStruct((RANGE, groups, LANES), f32),
            jax.ShapeDtypeStruct((RANGE, groups, LANES), f32),
            matrices,
            matrices,
        ),
        in_specs=[spec(VMEM)] * 9,
        out_specs=(spec(VMEM),) * 6,
        scratch_shapes=[
            pltpu.VMEM((rows + 2 * RANGE, cols), f32),
            pltpu.VMEM((4, bands, pixels), f32),
        ],
        compiler_params=pltpu.CompilerParams(vmem_limit_bytes=40 << 20),
        cost_estimate=pl.CostEstimate(flops=10**9, bytes_accessed=16 << 20, transcendentals=0),
        name="prepare",
    )(
        truth_field, truth_above, truth_below, truth_heads, truth_tails, truth_left, truth_right,
        neighbour_positions, unscaled_neighbour_factor,
    )

    side = jax.ShapeDtypeStruct((groups, members, LANES), f32)
    field, heads, tails = pl.pallas_call(
        regrid_kernel,
        out_shape=(jax.ShapeDtypeStruct((bands, members, pixels), f32), side, side),
        in_specs=[spec(SMEM), spec(VMEM), spec(VMEM), spec(VMEM)],
        out_specs=(spec(VMEM), spec(VMEM), spec(VMEM)),
        scratch_shapes=[pltpu.VMEM((4, bands, pixels), f32)],
        compiler_params=pltpu.CompilerParams(vmem_limit_bytes=32 << 20),
        name="regrid",
    )(place, incoming, neighbour_positions, unscaled_neighbour_factor)

    halo = 2 * RANGE
    above = shifted(field[bands - halo :], "tile", 1, False)
    below = shifted(field[:halo], "tile", -1, False)
    left_tails = shifted(tails, "face", 1, True)
    right_heads = shifted(heads, "face", -1, True)
    tile = lax.axis_index("tile")
    edge = jnp.stack(
        [RANGE - tile * rows, RANGE + (tile_count - tile) * rows]
    ).astype(jnp.int32)

    slots = pl.pallas_call(
        score_kernel,
        out_shape=jax.ShapeDtypeStruct((device_count, slot_count + 1, members, pixels), jnp.int16),
        in_specs=[spec(SMEM), spec(SMEM)] + [spec(VMEM)] * 11 + [spec(pl.ANY)] * 2,
        out_specs=spec(VMEM),
        scratch_shapes=[
            pltpu.VMEM((bands + 2 * halo, members, pixels), f32),
            pltpu.VMEM((bands + 2 * halo, members, pixels), f32),
            pltpu.VMEM((device_count, members, pixels), jnp.int32),
            pltpu.VMEM((bands, pixels, 2 * pixels), jnp.bfloat16),
            pltpu.VMEM((bands, pixels, 2 * pixels), jnp.bfloat16),
            pltpu.SemaphoreType.DMA((2,)),
        ],
        compiler_params=pltpu.CompilerParams(vmem_limit_bytes=40 << 20),
        name="score",
    )(
        edge, place, field, above, below, heads, tails, left_tails, right_heads,
        root_tall, root_wide, root_left, root_right, high, low,
    )
    returned = lax.all_to_all(
        slots, ("face", "tile"), split_axis=0, concat_axis=0, tiled=True
    )
    return pl.pallas_call(
        collect_kernel,
        out_shape=jax.ShapeDtypeStruct((members, bands, pixels), f32),
        in_specs=[spec(SMEM), spec(VMEM)],
        out_specs=spec(VMEM),
        scratch_shapes=[pltpu.VMEM((bands + 8, members, pixels), f32)],
        compiler_params=pltpu.CompilerParams(vmem_limit_bytes=32 << 20),
        name="collect",
    )(asked, returned)


def solution(mesh):
    in_specs = (
        P(None, ("face", "tile"), None),
        P(("face", "tile"), None),
        P(("face", "tile"), None),
        P(None, ("face", "tile"), None),
        P(None, ("face", "tile"), None),
        P("tile", "face"),
    )
    out_specs = P(None, ("face", "tile"), None)
    return jax.shard_map(local, mesh=mesh, in_specs=in_specs, out_specs=out_specs, check_vma=False)
```

```python
import functools

import jax
import jax.numpy as jnp
from jax import lax
from jax.experimental import pallas as pl
from jax.experimental.pallas import tpu as pltpu
from jax.sharding import PartitionSpec as P

RANGE = 8
FLOOR = 0.01
LANES = 128
STEPS = 32000.0
SHARE = 16384.0
VMEM = pltpu.VMEM
SMEM = pltpu.SMEM


def spec(space):
    return pl.BlockSpec(memory_space=space)


def root_of(diff):
    return lax.rsqrt(lax.rsqrt(diff * diff + FLOOR))


def lane_pick(values, index):
    return jnp.take_along_axis(values, index, axis=1, mode="promise_in_bounds")


def lane_ids():
    return lax.broadcasted_iota(jnp.int32, (16, LANES), 1)


def place_of(number, tiles):
    return (number // tiles, number % tiles)


def greet(count, tiles, me):
    barrier = pltpu.get_barrier_semaphore()

    def step(s, carry):
        other = (me + s) % count
        pl.semaphore_signal(
            barrier, inc=1, device_id=place_of(other, tiles), device_id_type=pl.DeviceIdType.MESH
        )
        return carry

    lax.fori_loop(1, count, step, 0)
    pl.semaphore_wait(barrier, count - 1)


def remote(source, target, sent, arrived, other, tiles):
    return pltpu.make_async_remote_copy(
        src_ref=source, dst_ref=target, send_sem=sent, recv_sem=arrived,
        device_id=place_of(other, tiles), device_id_type=pl.DeviceIdType.MESH,
    )


def fetch_kernel(
    count, tiles, wanted, strips, truth, heads, tails, positions, factors,
    incoming, asked, root_tall, root_wide, root_left, root_right, high_far, low_far,
    asked_rows, numbers, outgoing, list_sent, list_got, strip_sent, strip_got, local_sem,
    tall, left, right, high, low, weights, edge_sent, edge_got, stored,
):
    me = lax.axis_index("face") * tiles + lax.axis_index("tile")
    slot_count = outgoing.shape[1]
    bands = strips.shape[0]
    greet(count, tiles, me)

    def ask(s, carry):
        other = (me + s) % count
        remote(wanted.at[other], asked_rows.at[me], list_sent.at[s], list_got.at[s], other, tiles).start()
        return carry

    def heard(s, carry):
        other = (me + s) % count
        remote(wanted.at[other], asked_rows.at[me], list_sent.at[s], list_got.at[s], other, tiles).wait()
        return carry

    lax.fori_loop(1, count, ask, 0)
    asked_rows[me] = wanted[me]
    rows = truth.shape[0]
    faces = count // tiles
    face, tile = lax.axis_index("face"), lax.axis_index("tile")
    north = face * tiles + (tile + 1) % tiles
    south = face * tiles + (tile + tiles - 1) % tiles
    east = ((face + 1) % faces) * tiles + tile
    west = ((face + faces - 1) % faces) * tiles + tile
    edges = []
    for i, (source, target, other) in enumerate((
        (truth.at[pl.ds(rows - RANGE, RANGE)], tall.at[pl.ds(0, RANGE)], north),
        (truth.at[pl.ds(0, RANGE)], tall.at[pl.ds(rows + RANGE, RANGE)], south),
        (tails, left, east),
        (heads, right, west),
    )):
        edges.append(remote(source, target, edge_sent.at[i], edge_got.at[i], other, tiles))
    for edge in edges:
        edge.start()
    tall[pl.ds(RANGE, rows)] = truth[...]
    lax.fori_loop(1, count, heard, 0)
    listing = pltpu.make_async_copy(asked_rows, numbers, local_sem)
    listing.start()
    asked[...] = asked_rows[...]
    listing.wait()

    for k in range(slot_count):
        incoming[me, k] = strips[jnp.minimum(numbers[me, 0, k], bands - 1)]

    def send(s, carry):
        other = (me + s) % count
        for k in range(slot_count):
            outgoing[s, k] = strips[jnp.minimum(numbers[other, 0, k], bands - 1)]
        remote(outgoing.at[s], incoming.at[me], strip_sent.at[s], strip_got.at[s], other, tiles).start()
        return carry

    def got(s, carry):
        other = (me + s) % count
        remote(outgoing.at[s], incoming.at[me], strip_sent.at[s], strip_got.at[s], other, tiles).wait()
        return carry

    lax.fori_loop(1, count, send, 0)
    for edge in edges:
        edge.wait()
    prepare(
        truth, heads, tails, left, right, positions, factors,
        root_tall, root_wide, root_left, root_right, high, low, tall, weights,
    )
    store_high = pltpu.make_async_copy(high, high_far, stored.at[0])
    store_low = pltpu.make_async_copy(low, low_far, stored.at[1])
    store_high.start()
    store_low.start()
    lax.fori_loop(1, count, got, 0)
    store_high.wait()
    store_low.wait()


def regrid_kernel(place, incoming, positions, factors, field, heads, tails, weights):
    total = factors[0] + factors[1] + factors[2] + factors[3]
    for j in range(4):
        weights[j] = factors[j] / total
    members = field.shape[1]
    lane = lax.broadcasted_iota(jnp.int32, (members, LANES), 1)
    per_tile = LANES // RANGE
    for group in range(heads.shape[0]):
        def row_step(r, carry):
            head, tail = carry
            row = group * per_tile + r
            for half in range(2):
                g = 2 * row + half
                first = incoming[place[2 * g]].astype(jnp.float32)
                second = incoming[place[2 * g + 1]].astype(jnp.float32)
                summed = None
                for j in range(4):
                    at = jnp.broadcast_to(positions[j, pl.ds(g, 1), :], (members, LANES))
                    low = at & (LANES - 1)
                    picked = jnp.where(at < LANES, lane_pick(first, low), lane_pick(second, low))
                    term = picked * weights[j, pl.ds(g, 1), :]
                    summed = term if summed is None else summed + term
                field[g] = summed
                mine = (lane >> 3) == r
                if half == 0:
                    head = jnp.where(mine, pltpu.roll(summed, r * RANGE, 1), head)
                else:
                    tail = jnp.where(mine, pltpu.roll(summed, r * RANGE + RANGE, 1), tail)
            return head, tail

        zero = jnp.zeros((members, LANES), jnp.float32)
        head, tail = lax.fori_loop(0, per_tile, row_step, (zero, zero), unroll=2)
        heads[group] = head
        tails[group] = tail


def push_of(first, second, observed_root, scale):
    diff = first - second
    square = diff * diff + FLOOR
    inverse = lax.rsqrt(square)
    root = lax.rsqrt(inverse)
    spread = jnp.sum(root, axis=0, keepdims=True) * (1.0 / first.shape[0])
    mismatch = (observed_root - spread) * scale
    return mismatch * (diff * (root * inverse * inverse))


def prepare(
    truth, heads, tails, left, right, positions, factors,
    root_tall, root_wide, root_left, root_right, high, low, tall, weights,
):
    rows = truth.shape[0]
    span = rows + RANGE
    for k in range(1, RANGE + 1):
        root = root_of(tall[pl.ds(0, span), :] - tall[pl.ds(k, span), :])
        root_tall[2 * k - 2] = root[:, :LANES]
        root_tall[2 * k - 1] = root[:, LANES:]
        west, east = truth[:, :LANES], truth[:, LANES:]
        lane = lax.broadcasted_iota(jnp.int32, west.shape, 1)
        west_next = pltpu.roll(west, LANES - k, 1)
        east_next = pltpu.roll(east, LANES - k, 1)
        root_wide[2 * k - 2] = root_of(west - jnp.where(lane < LANES - k, west_next, east_next))
        root_wide[2 * k - 1] = root_of(east - east_next)
        shift = RANGE - k
        near = heads[...]
        far = right[...]
        if shift:
            near = jnp.concatenate([near[:, LANES - shift :], near[:, : LANES - shift]], axis=1)
            far = jnp.concatenate([far[:, LANES - shift :], far[:, : LANES - shift]], axis=1)
        root_left[k - 1] = root_of(left[...] - near)
        root_right[k - 1] = root_of(tails[...] - far)
    total = factors[0] + factors[1] + factors[2] + factors[3]
    for j in range(4):
        weights[j] = factors[j] / total
    spots = lax.broadcasted_iota(jnp.int32, (2 * LANES, LANES), 0)

    def step(g, carry):
        matrix = jnp.zeros((2 * LANES, LANES), jnp.float32)
        for j in range(4):
            at = positions[j, pl.ds(g, 1), :]
            matrix = matrix + jnp.where(spots == at, weights[j, pl.ds(g, 1), :], 0.0)
        matrix = matrix.T
        top = matrix.astype(jnp.bfloat16)
        high[g] = top
        low[g] = (matrix - top.astype(jnp.float32)).astype(jnp.bfloat16)
        return carry

    lax.fori_loop(0, high.shape[0], step, 0)


def score_kernel(
    edge, place, field, above, below, heads, tails, left_tails, right_heads,
    root_tall, root_wide, root_left, root_right, high_far, low_far,
    slots, ext, grad, scales, high, low, arrived,
):
    bands, members = field.shape[0], field.shape[1]
    rows = bands // 2
    halo = 2 * RANGE
    fetch_high = pltpu.make_async_copy(high_far, high, arrived.at[0])
    fetch_low = pltpu.make_async_copy(low_far, low, arrived.at[1])
    fetch_high.start()
    fetch_low.start()
    ext[pl.ds(0, halo)] = above[...]
    ext[pl.ds(halo, bands)] = field[...]
    ext[pl.ds(halo + bands, halo)] = below[...]
    grad[...] = jnp.zeros_like(grad)

    def tall_step(a, carry):
        for half in range(2):
            mine = ext[2 * a + half]
            own = jnp.zeros_like(mine)
            for k in range(1, RANGE + 1):
                inside = (a >= edge[0]) & (a + k < edge[1])
                scale = jnp.where(inside, 1.0 / (k * members), 0.0)
                other = 2 * (a + k) + half
                push = push_of(
                    mine, ext[other],
                    root_tall[2 * k - 2 + half, pl.ds(a, 1), :], scale,
                )
                own = own - push
                grad[other] = grad[other] + push
            grad[2 * a + half] = grad[2 * a + half] + own
        return carry

    lax.fori_loop(0, rows + RANGE, tall_step, 0)

    lane = lax.broadcasted_iota(jnp.int32, (members, LANES), 1)

    sub = lane & (RANGE - 1)
    per_tile = LANES // RANGE
    for group in range(heads.shape[0]):
        head, tail = heads[group], tails[group]
        left, right = left_tails[group], right_heads[group]
        head_grad = jnp.zeros_like(head)
        tail_grad = jnp.zeros_like(tail)
        for k in range(1, RANGE + 1):
            crossing = sub >= RANGE - k
            scale = 1.0 / (k * members)
            shift = RANGE - k
            moved = pltpu.roll(head, shift, 1) if shift else head
            push = push_of(left, moved, root_left[k - 1, pl.ds(group, 1), :], scale)
            push = jnp.where(crossing, push, 0.0)
            back = pltpu.roll(push, LANES - shift, 1) if shift else push
            head_grad = head_grad + back
            moved = pltpu.roll(right, shift, 1) if shift else right
            push = push_of(tail, moved, root_right[k - 1, pl.ds(group, 1), :], scale)
            tail_grad = tail_grad - jnp.where(crossing, push, 0.0)

        def spread_step(r, carry):
            g = halo + 2 * (group * per_tile + r)
            back = pltpu.roll(head_grad, LANES - r * RANGE, 1)
            grad[g] = grad[g] + jnp.where(lane < RANGE, back, 0.0)
            back = pltpu.roll(tail_grad, LANES - RANGE - r * RANGE, 1)
            grad[g + 1] = grad[g + 1] + jnp.where(lane >= LANES - RANGE, back, 0.0)
            return carry

        lax.fori_loop(0, per_tile, spread_step, 0)

    def wide_step(r, carry):
        g = 2 * r
        west, east = field[g], field[g + 1]
        west_grad, east_grad = grad[halo + g], grad[halo + g + 1]
        for k in range(1, RANGE + 1):
            scale = 1.0 / (k * members)
            within = lane < LANES - k
            after = lane >= k
            west_next = pltpu.roll(west, LANES - k, 1)
            east_next = pltpu.roll(east, LANES - k, 1)
            west_push = push_of(
                west, jnp.where(within, west_next, east_next),
                root_wide[2 * k - 2, pl.ds(r, 1), :], scale,
            )
            east_push = push_of(
                east, east_next, root_wide[2 * k - 1, pl.ds(r, 1), :], scale
            )
            east_push = jnp.where(within, east_push, 0.0)
            west_back = pltpu.roll(west_push, k, 1)
            east_back = pltpu.roll(east_push, k, 1)
            west_grad = west_grad - west_push + jnp.where(after, west_back, 0.0)
            east_grad = east_grad - east_push + jnp.where(after, east_back, west_back)
        for half, value in ((0, west_grad), (1, east_grad)):
            adjoint(g + half, value)
        return carry

    slot_count = slots.shape[1] - 1

    def adjoint(g, value):
        value_high = value.astype(jnp.bfloat16)
        value_low = (value - value_high.astype(jnp.float32)).astype(jnp.bfloat16)
        both = jnp.concatenate([value_high, value_low], axis=0)
        main = jnp.dot(both, high[g], preferred_element_type=jnp.float32)
        slope = (
            main[:members] + main[members:]
            + jnp.dot(value_high, low[g], preferred_element_type=jnp.float32)
        )
        for half in range(2):
            part = slope[:, half * LANES : (half + 1) * LANES]
            largest = jnp.max(jnp.abs(part), axis=1, keepdims=True)
            step = jnp.maximum(largest, 1e-30) * (1.0 / STEPS)
            code = jnp.round(part * (1.0 / step)).astype(jnp.int32)
            at = place[2 * g + half]
            holder = at // slot_count
            rank = at - holder * slot_count
            slots[holder, rank] = code.astype(jnp.int16)
            power = jnp.ceil(jnp.log2(step))
            share = jnp.round(step * jnp.exp2(-power) * SHARE)
            old = scales[holder]
            old = jnp.where(lane == rank, power.astype(jnp.int32), old)
            scales[holder] = jnp.where(lane == rank + LANES // 2, share.astype(jnp.int32), old)

    fetch_high.wait()
    fetch_low.wait()
    lax.fori_loop(0, rows, wide_step, 0)
    for holder in range(slots.shape[0]):
        slots[holder, slot_count] = scales[holder].astype(jnp.int16)


def collect_kernel(wanted, returned, slope, summed):
    bands = slope.shape[1]
    summed[...] = jnp.zeros_like(summed)

    slot_count = returned.shape[1] - 1

    def step(d, carry):
        scale = returned[d, slot_count].astype(jnp.int32).astype(jnp.float32)
        share = pltpu.roll(scale, LANES // 2, 1) * (1.0 / SHARE)
        step_of = share * jnp.exp2(scale)
        for k in range(slot_count):
            at = wanted[d * slot_count + k]
            code = returned[d, k].astype(jnp.int32).astype(jnp.float32)
            summed[at] = summed[at] + code * step_of[:, k : k + 1]
        return carry

    lax.fori_loop(0, returned.shape[0], step, 0, unroll=4)
    for g in range(bands):
        slope[:, g, :] = summed[g]


def halves(planes):
    return jnp.stack([p[:, at : at + LANES] for p in planes for at in (0, LANES)])


def shifted(cells, axis, step, closed):
    count = lax.axis_size(axis)
    ends = count if closed else count - 1
    pairs = [(i, (i + 1) % count) for i in range(ends)]
    if step < 0:
        pairs = [(b, a) for a, b in pairs]
    return lax.ppermute(cells, axis, pairs)


def local(
    predicted_field,
    parent_band_holder,
    parent_band_slot,
    neighbour_positions,
    unscaled_neighbour_factor,
    truth_field,
):
    members, bands, pixels = predicted_field.shape
    tile_count = lax.axis_size("tile")
    device_count = lax.axis_size(("face", "tile"))
    slot_count = max(2, 4 * bands // device_count)
    slots_all = device_count * slot_count
    rows, cols = bands // 2, 2 * pixels
    groups = rows * RANGE // LANES

    owner = parent_band_holder.reshape(-1)
    order = jnp.arange(2 * bands, dtype=jnp.int32)
    before = (owner[:, None] == owner[None, :]) & (order[None, :] < order[:, None])
    place = owner * slot_count + jnp.sum(before.astype(jnp.int32), axis=1)
    held = place[None, :] == jnp.arange(slots_all, dtype=jnp.int32)[:, None]
    wanted = bands + jnp.sum(
        jnp.where(held, parent_band_slot.reshape(-1)[None, :] - bands, 0), axis=1
    )
    strips = jnp.transpose(predicted_field, (1, 0, 2))
    lists = jnp.pad(
        wanted.reshape(device_count, 1, slot_count), ((0, 0), (0, 0), (0, LANES - slot_count))
    )
    truth_heads = truth_field[:, :RANGE].reshape(groups, LANES)
    truth_tails = truth_field[:, cols - RANGE :].reshape(groups, LANES)
    f32 = jnp.float32
    matrices = jax.ShapeDtypeStruct((bands, pixels, 2 * pixels), jnp.bfloat16)
    incoming, asked, root_tall, root_wide, root_left, root_right, high, low = pl.pallas_call(
        functools.partial(fetch_kernel, device_count, tile_count),
        out_shape=(
            jax.ShapeDtypeStruct((device_count, slot_count, members, pixels), predicted_field.dtype),
            jax.ShapeDtypeStruct((device_count, 1, LANES), jnp.int32),
            jax.ShapeDtypeStruct((2 * RANGE, rows + RANGE, LANES), f32),
            jax.ShapeDtypeStruct((2 * RANGE, rows, LANES), f32),
            jax.ShapeDtypeStruct((RANGE, groups, LANES), f32),
            jax.ShapeDtypeStruct((RANGE, groups, LANES), f32),
            matrices,
            matrices,
        ),
        in_specs=[spec(VMEM)] * 7,
        out_specs=(spec(VMEM),) * 6 + (spec(pl.ANY),) * 2,
        scratch_shapes=[
            pltpu.VMEM((device_count, 1, LANES), jnp.int32),
            pltpu.SMEM((device_count, 1, LANES), jnp.int32),
            pltpu.VMEM((device_count, slot_count, members, pixels), predicted_field.dtype),
            pltpu.SemaphoreType.DMA((device_count,)),
            pltpu.SemaphoreType.DMA((device_count,)),
            pltpu.SemaphoreType.DMA((device_count,)),
            pltpu.SemaphoreType.DMA((device_count,)),
            pltpu.SemaphoreType.DMA,
            pltpu.VMEM((rows + 2 * RANGE, cols), f32),
            pltpu.VMEM((groups, LANES), f32),
            pltpu.VMEM((groups, LANES), f32),
            pltpu.VMEM(matrices.shape, matrices.dtype),
            pltpu.VMEM(matrices.shape, matrices.dtype),
            pltpu.VMEM((4, bands, pixels), f32),
            pltpu.SemaphoreType.DMA((4,)),
            pltpu.SemaphoreType.DMA((4,)),
            pltpu.SemaphoreType.DMA((2,)),
        ],
        compiler_params=pltpu.CompilerParams(
            collective_id=1, has_side_effects=True, vmem_limit_bytes=40 << 20
        ),
        name="fetch",
    )(
        lists, strips, truth_field, truth_heads, truth_tails,
        neighbour_positions, unscaled_neighbour_factor,
    )
    incoming = incoming.reshape(slots_all, members, pixels)
    asked = asked[:, 0, :slot_count].reshape(-1)

    side = jax.ShapeDtypeStruct((groups, members, LANES), f32)
    field, heads, tails = pl.pallas_call(
        regrid_kernel,
        out_shape=(jax.ShapeDtypeStruct((bands, members, pixels), f32), side, side),
        in_specs=[spec(SMEM), spec(VMEM), spec(VMEM), spec(VMEM)],
        out_specs=(spec(VMEM), spec(VMEM), spec(VMEM)),
        scratch_shapes=[pltpu.VMEM((4, bands, pixels), f32)],
        compiler_params=pltpu.CompilerParams(vmem_limit_bytes=32 << 20),
        name="regrid",
    )(place, incoming, neighbour_positions, unscaled_neighbour_factor)

    halo = 2 * RANGE
    above = shifted(field[bands - halo :], "tile", 1, False)
    below = shifted(field[:halo], "tile", -1, False)
    left_tails = shifted(tails, "face", 1, True)
    right_heads = shifted(heads, "face", -1, True)
    tile = lax.axis_index("tile")
    edge = jnp.stack(
        [RANGE - tile * rows, RANGE + (tile_count - tile) * rows]
    ).astype(jnp.int32)

    slots = pl.pallas_call(
        score_kernel,
        out_shape=jax.ShapeDtypeStruct((device_count, slot_count + 1, members, pixels), jnp.int16),
        in_specs=[spec(SMEM), spec(SMEM)] + [spec(VMEM)] * 11 + [spec(pl.ANY)] * 2,
        out_specs=spec(VMEM),
        scratch_shapes=[
            pltpu.VMEM((bands + 2 * halo, members, pixels), f32),
            pltpu.VMEM((bands + 2 * halo, members, pixels), f32),
            pltpu.VMEM((device_count, members, pixels), jnp.int32),
            pltpu.VMEM((bands, pixels, 2 * pixels), jnp.bfloat16),
            pltpu.VMEM((bands, pixels, 2 * pixels), jnp.bfloat16),
            pltpu.SemaphoreType.DMA((2,)),
        ],
        compiler_params=pltpu.CompilerParams(vmem_limit_bytes=40 << 20),
        name="score",
    )(
        edge, place, field, above, below, heads, tails, left_tails, right_heads,
        root_tall, root_wide, root_left, root_right, high, low,
    )
    returned = lax.all_to_all(
        slots, ("face", "tile"), split_axis=0, concat_axis=0, tiled=True
    )
    return pl.pallas_call(
        collect_kernel,
        out_shape=jax.ShapeDtypeStruct((members, bands, pixels), f32),
        in_specs=[spec(SMEM), spec(VMEM)],
        out_specs=spec(VMEM),
        scratch_shapes=[pltpu.VMEM((bands + 8, members, pixels), f32)],
        compiler_params=pltpu.CompilerParams(vmem_limit_bytes=32 << 20),
        name="collect",
    )(asked, returned)


def solution(mesh):
    in_specs = (
        P(None, ("face", "tile"), None),
        P(("face", "tile"), None),
        P(("face", "tile"), None),
        P(None, ("face", "tile"), None),
        P(None, ("face", "tile"), None),
        P("tile", "face"),
    )
    out_specs = P(None, ("face", "tile"), None)
    return jax.shard_map(local, mesh=mesh, in_specs=in_specs, out_specs=out_specs, check_vma=False)
```

```python
import functools

import jax
import jax.numpy as jnp
from jax import lax
from jax.experimental import pallas as pl
from jax.experimental.pallas import tpu as pltpu
from jax.sharding import PartitionSpec as P

RANGE = 8
FLOOR = 0.01
LANES = 128
STEPS = 32000.0
SHARE = 16384.0
VMEM = pltpu.VMEM
SMEM = pltpu.SMEM


def spec(space):
    return pl.BlockSpec(memory_space=space)


def root_of(diff):
    return lax.rsqrt(lax.rsqrt(diff * diff + FLOOR))


def lane_pick(values, index):
    return jnp.take_along_axis(values, index, axis=1, mode="promise_in_bounds")


def lane_ids():
    return lax.broadcasted_iota(jnp.int32, (16, LANES), 1)


def place_of(number, tiles):
    return (number // tiles, number % tiles)


def greet(count, tiles, me):
    barrier = pltpu.get_barrier_semaphore()

    def step(s, carry):
        other = (me + s) % count
        pl.semaphore_signal(
            barrier, inc=1, device_id=place_of(other, tiles), device_id_type=pl.DeviceIdType.MESH
        )
        return carry

    lax.fori_loop(1, count, step, 0)
    pl.semaphore_wait(barrier, count - 1)


def remote(source, target, sent, arrived, other, tiles):
    return pltpu.make_async_remote_copy(
        src_ref=source, dst_ref=target, send_sem=sent, recv_sem=arrived,
        device_id=place_of(other, tiles), device_id_type=pl.DeviceIdType.MESH,
    )


def fetch_kernel(
    count, tiles, wanted, strips, truth, heads, tails, positions, factors,
    incoming, asked, root_tall, root_wide, root_left, root_right, high_far, low_far,
    asked_rows, numbers, outgoing, list_sent, list_got, strip_sent, strip_got, local_sem,
    tall, left, right, high, low, weights, edge_sent, edge_got, stored,
):
    me = lax.axis_index("face") * tiles + lax.axis_index("tile")
    slot_count = outgoing.shape[1]
    bands = strips.shape[0]
    greet(count, tiles, me)

    def ask(s, carry):
        other = (me + s) % count
        remote(wanted.at[other], asked_rows.at[me], list_sent.at[s], list_got.at[s], other, tiles).start()
        return carry

    def heard(s, carry):
        other = (me + s) % count
        remote(wanted.at[other], asked_rows.at[me], list_sent.at[s], list_got.at[s], other, tiles).wait()
        return carry

    lax.fori_loop(1, count, ask, 0)
    asked_rows[me] = wanted[me]
    rows = truth.shape[0]
    faces = count // tiles
    face, tile = lax.axis_index("face"), lax.axis_index("tile")
    north = face * tiles + (tile + 1) % tiles
    south = face * tiles + (tile + tiles - 1) % tiles
    east = ((face + 1) % faces) * tiles + tile
    west = ((face + faces - 1) % faces) * tiles + tile
    edges = []
    for i, (source, target, other) in enumerate((
        (truth.at[pl.ds(rows - RANGE, RANGE)], tall.at[pl.ds(0, RANGE)], north),
        (truth.at[pl.ds(0, RANGE)], tall.at[pl.ds(rows + RANGE, RANGE)], south),
        (tails, left, east),
        (heads, right, west),
    )):
        edges.append(remote(source, target, edge_sent.at[i], edge_got.at[i], other, tiles))
    for edge in edges:
        edge.start()
    tall[pl.ds(RANGE, rows)] = truth[...]
    lax.fori_loop(1, count, heard, 0)
    listing = pltpu.make_async_copy(asked_rows, numbers, local_sem)
    listing.start()
    asked[...] = asked_rows[...]
    listing.wait()

    for k in range(slot_count):
        incoming[me, k] = strips[jnp.minimum(numbers[me, 0, k], bands - 1)]

    def send(s, carry):
        other = (me + s) % count
        for k in range(slot_count):
            outgoing[s, k] = strips[jnp.minimum(numbers[other, 0, k], bands - 1)]
        remote(outgoing.at[s], incoming.at[me], strip_sent.at[s], strip_got.at[s], other, tiles).start()
        return carry

    def got(s, carry):
        other = (me + s) % count
        remote(outgoing.at[s], incoming.at[me], strip_sent.at[s], strip_got.at[s], other, tiles).wait()
        return carry

    lax.fori_loop(1, count, send, 0)
    for edge in edges:
        edge.wait()
    prepare(
        truth, heads, tails, left, right, positions, factors,
        root_tall, root_wide, root_left, root_right, high, low, tall, weights,
    )
    store_high = pltpu.make_async_copy(high, high_far, stored.at[0])
    store_low = pltpu.make_async_copy(low, low_far, stored.at[1])
    store_high.start()
    store_low.start()
    lax.fori_loop(1, count, got, 0)
    store_high.wait()
    store_low.wait()


def sides(count, tiles):
    faces = count // tiles
    face, tile = lax.axis_index("face"), lax.axis_index("tile")
    return (
        face * tiles + (tile + 1) % tiles,
        face * tiles + (tile + tiles - 1) % tiles,
        ((face + 1) % faces) * tiles + tile,
        ((face + faces - 1) % faces) * tiles + tile,
    )


def halo_kernel(count, tiles, field, heads, tails, above, below, left, right, sent, got):
    bands, halo = field.shape[0], above.shape[0]
    others = sides(count, tiles)
    barrier = pltpu.get_barrier_semaphore()
    for other in others:
        pl.semaphore_signal(
            barrier, inc=1, device_id=place_of(other, tiles), device_id_type=pl.DeviceIdType.MESH
        )
    pl.semaphore_wait(barrier, 4)
    copies = []
    for i, (source, target) in enumerate((
        (field.at[pl.ds(bands - halo, halo)], above),
        (field.at[pl.ds(0, halo)], below),
        (tails, left),
        (heads, right),
    )):
        copies.append(remote(source, target, sent.at[i], got.at[i], others[i], tiles))
    for copy in copies:
        copy.start()
    for copy in copies:
        copy.wait()


def return_kernel(count, tiles, slots, returned, sent, got):
    me = lax.axis_index("face") * tiles + lax.axis_index("tile")
    greet(count, tiles, me)

    def send(s, carry):
        other = (me + s) % count
        remote(slots.at[other], returned.at[me], sent.at[s], got.at[s], other, tiles).start()
        return carry

    def wait(s, carry):
        other = (me + s) % count
        remote(slots.at[other], returned.at[me], sent.at[s], got.at[s], other, tiles).wait()
        return carry

    lax.fori_loop(1, count, send, 0)
    returned[me] = slots[me]
    lax.fori_loop(1, count, wait, 0)


def regrid_kernel(place, incoming, positions, factors, field, heads, tails, weights):
    total = factors[0] + factors[1] + factors[2] + factors[3]
    for j in range(4):
        weights[j] = factors[j] / total
    members = field.shape[1]
    lane = lax.broadcasted_iota(jnp.int32, (members, LANES), 1)
    per_tile = LANES // RANGE
    for group in range(heads.shape[0]):
        def row_step(r, carry):
            head, tail = carry
            row = group * per_tile + r
            for half in range(2):
                g = 2 * row + half
                first = incoming[place[2 * g]].astype(jnp.float32)
                second = incoming[place[2 * g + 1]].astype(jnp.float32)
                summed = None
                for j in range(4):
                    at = jnp.broadcast_to(positions[j, pl.ds(g, 1), :], (members, LANES))
                    low = at & (LANES - 1)
                    picked = jnp.where(at < LANES, lane_pick(first, low), lane_pick(second, low))
                    term = picked * weights[j, pl.ds(g, 1), :]
                    summed = term if summed is None else summed + term
                field[g] = summed
                mine = (lane >> 3) == r
                if half == 0:
                    head = jnp.where(mine, pltpu.roll(summed, r * RANGE, 1), head)
                else:
                    tail = jnp.where(mine, pltpu.roll(summed, r * RANGE + RANGE, 1), tail)
            return head, tail

        zero = jnp.zeros((members, LANES), jnp.float32)
        head, tail = lax.fori_loop(0, per_tile, row_step, (zero, zero), unroll=2)
        heads[group] = head
        tails[group] = tail


def push_of(first, second, observed_root, scale):
    diff = first - second
    square = diff * diff + FLOOR
    inverse = lax.rsqrt(square)
    root = lax.rsqrt(inverse)
    spread = jnp.sum(root, axis=0, keepdims=True) * (1.0 / first.shape[0])
    mismatch = (observed_root - spread) * scale
    return mismatch * (diff * (root * inverse * inverse))


def prepare(
    truth, heads, tails, left, right, positions, factors,
    root_tall, root_wide, root_left, root_right, high, low, tall, weights,
):
    rows = truth.shape[0]
    span = rows + RANGE
    for k in range(1, RANGE + 1):
        root = root_of(tall[pl.ds(0, span), :] - tall[pl.ds(k, span), :])
        root_tall[2 * k - 2] = root[:, :LANES]
        root_tall[2 * k - 1] = root[:, LANES:]
        west, east = truth[:, :LANES], truth[:, LANES:]
        lane = lax.broadcasted_iota(jnp.int32, west.shape, 1)
        west_next = pltpu.roll(west, LANES - k, 1)
        east_next = pltpu.roll(east, LANES - k, 1)
        root_wide[2 * k - 2] = root_of(west - jnp.where(lane < LANES - k, west_next, east_next))
        root_wide[2 * k - 1] = root_of(east - east_next)
        shift = RANGE - k
        near = heads[...]
        far = right[...]
        if shift:
            near = jnp.concatenate([near[:, LANES - shift :], near[:, : LANES - shift]], axis=1)
            far = jnp.concatenate([far[:, LANES - shift :], far[:, : LANES - shift]], axis=1)
        root_left[k - 1] = root_of(left[...] - near)
        root_right[k - 1] = root_of(tails[...] - far)
    total = factors[0] + factors[1] + factors[2] + factors[3]
    for j in range(4):
        weights[j] = factors[j] / total
    spots = lax.broadcasted_iota(jnp.int32, (2 * LANES, LANES), 0)

    def step(g, carry):
        matrix = jnp.zeros((2 * LANES, LANES), jnp.float32)
        for j in range(4):
            at = positions[j, pl.ds(g, 1), :]
            matrix = matrix + jnp.where(spots == at, weights[j, pl.ds(g, 1), :], 0.0)
        matrix = matrix.T
        top = matrix.astype(jnp.bfloat16)
        high[g] = top
        low[g] = (matrix - top.astype(jnp.float32)).astype(jnp.bfloat16)
        return carry

    lax.fori_loop(0, high.shape[0], step, 0)


def score_kernel(
    edge, place, field, above, below, heads, tails, left_tails, right_heads,
    root_tall, root_wide, root_left, root_right, high_far, low_far,
    slots, ext, grad, scales, high, low, arrived,
):
    bands, members = field.shape[0], field.shape[1]
    rows = bands // 2
    halo = 2 * RANGE
    fetch_high = pltpu.make_async_copy(high_far, high, arrived.at[0])
    fetch_low = pltpu.make_async_copy(low_far, low, arrived.at[1])
    fetch_high.start()
    fetch_low.start()
    ext[pl.ds(0, halo)] = above[...]
    ext[pl.ds(halo, bands)] = field[...]
    ext[pl.ds(halo + bands, halo)] = below[...]
    grad[...] = jnp.zeros_like(grad)

    def tall_step(a, carry):
        for half in range(2):
            mine = ext[2 * a + half]
            own = jnp.zeros_like(mine)
            for k in range(1, RANGE + 1):
                inside = (a >= edge[0]) & (a + k < edge[1])
                scale = jnp.where(inside, 1.0 / (k * members), 0.0)
                other = 2 * (a + k) + half
                push = push_of(
                    mine, ext[other],
                    root_tall[2 * k - 2 + half, pl.ds(a, 1), :], scale,
                )
                own = own - push
                grad[other] = grad[other] + push
            grad[2 * a + half] = grad[2 * a + half] + own
        return carry

    lax.fori_loop(0, rows + RANGE, tall_step, 0)

    lane = lax.broadcasted_iota(jnp.int32, (members, LANES), 1)

    sub = lane & (RANGE - 1)
    per_tile = LANES // RANGE
    for group in range(heads.shape[0]):
        head, tail = heads[group], tails[group]
        left, right = left_tails[group], right_heads[group]
        head_grad = jnp.zeros_like(head)
        tail_grad = jnp.zeros_like(tail)
        for k in range(1, RANGE + 1):
            crossing = sub >= RANGE - k
            scale = 1.0 / (k * members)
            shift = RANGE - k
            moved = pltpu.roll(head, shift, 1) if shift else head
            push = push_of(left, moved, root_left[k - 1, pl.ds(group, 1), :], scale)
            push = jnp.where(crossing, push, 0.0)
            back = pltpu.roll(push, LANES - shift, 1) if shift else push
            head_grad = head_grad + back
            moved = pltpu.roll(right, shift, 1) if shift else right
            push = push_of(tail, moved, root_right[k - 1, pl.ds(group, 1), :], scale)
            tail_grad = tail_grad - jnp.where(crossing, push, 0.0)

        def spread_step(r, carry):
            g = halo + 2 * (group * per_tile + r)
            back = pltpu.roll(head_grad, LANES - r * RANGE, 1)
            grad[g] = grad[g] + jnp.where(lane < RANGE, back, 0.0)
            back = pltpu.roll(tail_grad, LANES - RANGE - r * RANGE, 1)
            grad[g + 1] = grad[g + 1] + jnp.where(lane >= LANES - RANGE, back, 0.0)
            return carry

        lax.fori_loop(0, per_tile, spread_step, 0)

    def wide_step(r, carry):
        g = 2 * r
        west, east = field[g], field[g + 1]
        west_grad, east_grad = grad[halo + g], grad[halo + g + 1]
        for k in range(1, RANGE + 1):
            scale = 1.0 / (k * members)
            within = lane < LANES - k
            after = lane >= k
            west_next = pltpu.roll(west, LANES - k, 1)
            east_next = pltpu.roll(east, LANES - k, 1)
            west_push = push_of(
                west, jnp.where(within, west_next, east_next),
                root_wide[2 * k - 2, pl.ds(r, 1), :], scale,
            )
            east_push = push_of(
                east, east_next, root_wide[2 * k - 1, pl.ds(r, 1), :], scale
            )
            east_push = jnp.where(within, east_push, 0.0)
            west_back = pltpu.roll(west_push, k, 1)
            east_back = pltpu.roll(east_push, k, 1)
            west_grad = west_grad - west_push + jnp.where(after, west_back, 0.0)
            east_grad = east_grad - east_push + jnp.where(after, east_back, west_back)
        for half, value in ((0, west_grad), (1, east_grad)):
            adjoint(g + half, value)
        return carry

    slot_count = slots.shape[1] - 1

    def adjoint(g, value):
        value_high = value.astype(jnp.bfloat16)
        value_low = (value - value_high.astype(jnp.float32)).astype(jnp.bfloat16)
        both = jnp.concatenate([value_high, value_low], axis=0)
        main = jnp.dot(both, high[g], preferred_element_type=jnp.float32)
        slope = (
            main[:members] + main[members:]
            + jnp.dot(value_high, low[g], preferred_element_type=jnp.float32)
        )
        for half in range(2):
            part = slope[:, half * LANES : (half + 1) * LANES]
            largest = jnp.max(jnp.abs(part), axis=1, keepdims=True)
            step = jnp.maximum(largest, 1e-30) * (1.0 / STEPS)
            code = jnp.round(part * (1.0 / step)).astype(jnp.int32)
            at = place[2 * g + half]
            holder = at // slot_count
            rank = at - holder * slot_count
            slots[holder, rank] = code.astype(jnp.int16)
            power = jnp.ceil(jnp.log2(step))
            share = jnp.round(step * jnp.exp2(-power) * SHARE)
            old = scales[holder]
            old = jnp.where(lane == rank, power.astype(jnp.int32), old)
            scales[holder] = jnp.where(lane == rank + LANES // 2, share.astype(jnp.int32), old)

    fetch_high.wait()
    fetch_low.wait()
    lax.fori_loop(0, rows, wide_step, 0)
    for holder in range(slots.shape[0]):
        slots[holder, slot_count] = scales[holder].astype(jnp.int16)


def collect_kernel(wanted, returned, slope, summed):
    bands = slope.shape[1]
    summed[...] = jnp.zeros_like(summed)

    slot_count = returned.shape[1] - 1

    def step(d, carry):
        scale = returned[d, slot_count].astype(jnp.int32).astype(jnp.float32)
        share = pltpu.roll(scale, LANES // 2, 1) * (1.0 / SHARE)
        step_of = share * jnp.exp2(scale)
        for k in range(slot_count):
            at = wanted[d * slot_count + k]
            code = returned[d, k].astype(jnp.int32).astype(jnp.float32)
            summed[at] = summed[at] + code * step_of[:, k : k + 1]
        return carry

    lax.fori_loop(0, returned.shape[0], step, 0, unroll=4)
    for g in range(bands):
        slope[:, g, :] = summed[g]


def local(
    predicted_field,
    parent_band_holder,
    parent_band_slot,
    neighbour_positions,
    unscaled_neighbour_factor,
    truth_field,
):
    members, bands, pixels = predicted_field.shape
    tile_count = lax.axis_size("tile")
    device_count = lax.axis_size(("face", "tile"))
    slot_count = max(2, 4 * bands // device_count)
    slots_all = device_count * slot_count
    rows, cols = bands // 2, 2 * pixels
    groups = rows * RANGE // LANES

    owner = parent_band_holder.reshape(-1)
    order = jnp.arange(2 * bands, dtype=jnp.int32)
    before = (owner[:, None] == owner[None, :]) & (order[None, :] < order[:, None])
    place = owner * slot_count + jnp.sum(before.astype(jnp.int32), axis=1)
    held = place[None, :] == jnp.arange(slots_all, dtype=jnp.int32)[:, None]
    wanted = bands + jnp.sum(
        jnp.where(held, parent_band_slot.reshape(-1)[None, :] - bands, 0), axis=1
    )
    strips = jnp.transpose(predicted_field, (1, 0, 2))
    lists = jnp.pad(
        wanted.reshape(device_count, 1, slot_count), ((0, 0), (0, 0), (0, LANES - slot_count))
    )
    truth_heads = truth_field[:, :RANGE].reshape(groups, LANES)
    truth_tails = truth_field[:, cols - RANGE :].reshape(groups, LANES)
    f32 = jnp.float32
    matrices = jax.ShapeDtypeStruct((bands, pixels, 2 * pixels), jnp.bfloat16)
    incoming, asked, root_tall, root_wide, root_left, root_right, high, low = pl.pallas_call(
        functools.partial(fetch_kernel, device_count, tile_count),
        out_shape=(
            jax.ShapeDtypeStruct((device_count, slot_count, members, pixels), predicted_field.dtype),
            jax.ShapeDtypeStruct((device_count, 1, LANES), jnp.int32),
            jax.ShapeDtypeStruct((2 * RANGE, rows + RANGE, LANES), f32),
            jax.ShapeDtypeStruct((2 * RANGE, rows, LANES), f32),
            jax.ShapeDtypeStruct((RANGE, groups, LANES), f32),
            jax.ShapeDtypeStruct((RANGE, groups, LANES), f32),
            matrices,
            matrices,
        ),
        in_specs=[spec(VMEM)] * 7,
        out_specs=(spec(VMEM),) * 6 + (spec(pl.ANY),) * 2,
        scratch_shapes=[
            pltpu.VMEM((device_count, 1, LANES), jnp.int32),
            pltpu.SMEM((device_count, 1, LANES), jnp.int32),
            pltpu.VMEM((device_count, slot_count, members, pixels), predicted_field.dtype),
            pltpu.SemaphoreType.DMA((device_count,)),
            pltpu.SemaphoreType.DMA((device_count,)),
            pltpu.SemaphoreType.DMA((device_count,)),
            pltpu.SemaphoreType.DMA((device_count,)),
            pltpu.SemaphoreType.DMA,
            pltpu.VMEM((rows + 2 * RANGE, cols), f32),
            pltpu.VMEM((groups, LANES), f32),
            pltpu.VMEM((groups, LANES), f32),
            pltpu.VMEM(matrices.shape, matrices.dtype),
            pltpu.VMEM(matrices.shape, matrices.dtype),
            pltpu.VMEM((4, bands, pixels), f32),
            pltpu.SemaphoreType.DMA((4,)),
            pltpu.SemaphoreType.DMA((4,)),
            pltpu.SemaphoreType.DMA((2,)),
        ],
        compiler_params=pltpu.CompilerParams(
            collective_id=1, has_side_effects=True, vmem_limit_bytes=56 << 20
        ),
        name="fetch",
    )(
        lists, strips, truth_field, truth_heads, truth_tails,
        neighbour_positions, unscaled_neighbour_factor,
    )
    incoming = incoming.reshape(slots_all, members, pixels)
    asked = asked[:, 0, :slot_count].reshape(-1)

    side = jax.ShapeDtypeStruct((groups, members, LANES), f32)
    field, heads, tails = pl.pallas_call(
        regrid_kernel,
        out_shape=(jax.ShapeDtypeStruct((bands, members, pixels), f32), side, side),
        in_specs=[spec(SMEM), spec(VMEM), spec(VMEM), spec(VMEM)],
        out_specs=(spec(VMEM), spec(VMEM), spec(VMEM)),
        scratch_shapes=[pltpu.VMEM((4, bands, pixels), f32)],
        compiler_params=pltpu.CompilerParams(vmem_limit_bytes=56 << 20),
        name="regrid",
    )(place, incoming, neighbour_positions, unscaled_neighbour_factor)

    halo = 2 * RANGE
    strip_halo = jax.ShapeDtypeStruct((halo, members, pixels), f32)
    above, below, left_tails, right_heads = pl.pallas_call(
        functools.partial(halo_kernel, device_count, tile_count),
        out_shape=(strip_halo, strip_halo, side, side),
        in_specs=[spec(VMEM)] * 3,
        out_specs=(spec(VMEM),) * 4,
        scratch_shapes=[pltpu.SemaphoreType.DMA((4,)), pltpu.SemaphoreType.DMA((4,))],
        compiler_params=pltpu.CompilerParams(
            collective_id=2, has_side_effects=True, vmem_limit_bytes=56 << 20
        ),
        name="halo",
    )(field, heads, tails)
    tile = lax.axis_index("tile")
    edge = jnp.stack(
        [RANGE - tile * rows, RANGE + (tile_count - tile) * rows]
    ).astype(jnp.int32)

    slots = pl.pallas_call(
        score_kernel,
        out_shape=jax.ShapeDtypeStruct((device_count, slot_count + 1, members, pixels), jnp.int16),
        in_specs=[spec(SMEM), spec(SMEM)] + [spec(VMEM)] * 11 + [spec(pl.ANY)] * 2,
        out_specs=spec(VMEM),
        scratch_shapes=[
            pltpu.VMEM((bands + 2 * halo, members, pixels), f32),
            pltpu.VMEM((bands + 2 * halo, members, pixels), f32),
            pltpu.VMEM((device_count, members, pixels), jnp.int32),
            pltpu.VMEM((bands, pixels, 2 * pixels), jnp.bfloat16),
            pltpu.VMEM((bands, pixels, 2 * pixels), jnp.bfloat16),
            pltpu.SemaphoreType.DMA((2,)),
        ],
        compiler_params=pltpu.CompilerParams(vmem_limit_bytes=56 << 20),
        name="score",
    )(
        edge, place, field, above, below, heads, tails, left_tails, right_heads,
        root_tall, root_wide, root_left, root_right, high, low,
    )
    returned = pl.pallas_call(
        functools.partial(return_kernel, device_count, tile_count),
        out_shape=jax.ShapeDtypeStruct(slots.shape, slots.dtype),
        in_specs=[spec(VMEM)],
        out_specs=spec(VMEM),
        scratch_shapes=[
            pltpu.SemaphoreType.DMA((device_count,)),
            pltpu.SemaphoreType.DMA((device_count,)),
        ],
        compiler_params=pltpu.CompilerParams(
            collective_id=3, has_side_effects=True, vmem_limit_bytes=56 << 20
        ),
        name="give_back",
    )(slots)
    return pl.pallas_call(
        collect_kernel,
        out_shape=jax.ShapeDtypeStruct((members, bands, pixels), f32),
        in_specs=[spec(SMEM), spec(VMEM)],
        out_specs=spec(VMEM),
        scratch_shapes=[pltpu.VMEM((bands + 8, members, pixels), f32)],
        compiler_params=pltpu.CompilerParams(vmem_limit_bytes=56 << 20),
        name="collect",
    )(asked, returned)


def solution(mesh):
    in_specs = (
        P(None, ("face", "tile"), None),
        P(("face", "tile"), None),
        P(("face", "tile"), None),
        P(None, ("face", "tile"), None),
        P(None, ("face", "tile"), None),
        P("tile", "face"),
    )
    out_specs = P(None, ("face", "tile"), None)
    return jax.shard_map(local, mesh=mesh, in_specs=in_specs, out_specs=out_specs, check_vma=False)
```

```python
import functools

import jax
import jax.numpy as jnp
from jax import lax
from jax.experimental import pallas as pl
from jax.experimental.pallas import tpu as pltpu
from jax.sharding import PartitionSpec as P

RANGE = 8
FLOOR = 0.01
LANES = 128
STEPS = 32000.0
SHARE = 16384.0
VMEM = pltpu.VMEM
SMEM = pltpu.SMEM


def spec(space):
    return pl.BlockSpec(memory_space=space)


def root_of(diff):
    return lax.rsqrt(lax.rsqrt(diff * diff + FLOOR))


def lane_pick(values, index):
    return jnp.take_along_axis(values, index, axis=1, mode="promise_in_bounds")


def lane_ids():
    return lax.broadcasted_iota(jnp.int32, (16, LANES), 1)


def place_of(number, tiles):
    return (number // tiles, number % tiles)


def greet(count, tiles, me):
    barrier = pltpu.get_barrier_semaphore()

    def step(s, carry):
        other = (me + s) % count
        pl.semaphore_signal(
            barrier, inc=1, device_id=place_of(other, tiles), device_id_type=pl.DeviceIdType.MESH
        )
        return carry

    lax.fori_loop(1, count, step, 0)
    pl.semaphore_wait(barrier, count - 1)


def remote(source, target, sent, arrived, other, tiles):
    return pltpu.make_async_remote_copy(
        src_ref=source, dst_ref=target, send_sem=sent, recv_sem=arrived,
        device_id=place_of(other, tiles), device_id_type=pl.DeviceIdType.MESH,
    )


def fetch_kernel(
    count, tiles, wanted, strips, truth, heads, tails, positions, factors,
    incoming, asked, root_tall, root_wide, root_left, root_right, high_far, low_far,
    asked_rows, numbers, outgoing, list_sent, list_got, strip_sent, strip_got, local_sem,
    tall, left, right, high, low, weights, edge_sent, edge_got, stored,
):
    me = lax.axis_index("face") * tiles + lax.axis_index("tile")
    slot_count = outgoing.shape[1]
    bands = strips.shape[0]
    greet(count, tiles, me)

    def ask(s, carry):
        other = (me + s) % count
        remote(wanted.at[other], asked_rows.at[me], list_sent.at[s], list_got.at[s], other, tiles).start()
        return carry

    def heard(s, carry):
        other = (me + s) % count
        remote(wanted.at[other], asked_rows.at[me], list_sent.at[s], list_got.at[s], other, tiles).wait()
        return carry

    lax.fori_loop(1, count, ask, 0)
    asked_rows[me] = wanted[me]
    rows = truth.shape[0]
    faces = count // tiles
    face, tile = lax.axis_index("face"), lax.axis_index("tile")
    north = face * tiles + (tile + 1) % tiles
    south = face * tiles + (tile + tiles - 1) % tiles
    east = ((face + 1) % faces) * tiles + tile
    west = ((face + faces - 1) % faces) * tiles + tile
    edges = []
    for i, (source, target, other) in enumerate((
        (truth.at[pl.ds(rows - RANGE, RANGE)], tall.at[pl.ds(0, RANGE)], north),
        (truth.at[pl.ds(0, RANGE)], tall.at[pl.ds(rows + RANGE, RANGE)], south),
        (tails, left, east),
        (heads, right, west),
    )):
        edges.append(remote(source, target, edge_sent.at[i], edge_got.at[i], other, tiles))
    for edge in edges:
        edge.start()
    tall[pl.ds(RANGE, rows)] = truth[...]
    lax.fori_loop(1, count, heard, 0)
    listing = pltpu.make_async_copy(asked_rows, numbers, local_sem)
    listing.start()
    asked[...] = asked_rows[...]
    listing.wait()

    for k in range(slot_count):
        incoming[me, k] = strips[jnp.minimum(numbers[me, 0, k], bands - 1)]

    def send(s, carry):
        other = (me + s) % count
        for k in range(slot_count):
            outgoing[s, k] = strips[jnp.minimum(numbers[other, 0, k], bands - 1)]
        remote(outgoing.at[s], incoming.at[me], strip_sent.at[s], strip_got.at[s], other, tiles).start()
        return carry

    def got(s, carry):
        other = (me + s) % count
        remote(outgoing.at[s], incoming.at[me], strip_sent.at[s], strip_got.at[s], other, tiles).wait()
        return carry

    lax.fori_loop(1, count, send, 0)
    for edge in edges:
        edge.wait()
    prepare(
        truth, heads, tails, left, right, positions, factors,
        root_tall, root_wide, root_left, root_right, high, low, tall, weights,
    )
    store_high = pltpu.make_async_copy(high, high_far, stored.at[0])
    store_low = pltpu.make_async_copy(low, low_far, stored.at[1])
    store_high.start()
    store_low.start()
    lax.fori_loop(1, count, got, 0)
    store_high.wait()
    store_low.wait()


def sides(count, tiles):
    faces = count // tiles
    face, tile = lax.axis_index("face"), lax.axis_index("tile")
    return (
        face * tiles + (tile + 1) % tiles,
        face * tiles + (tile + tiles - 1) % tiles,
        ((face + 1) % faces) * tiles + tile,
        ((face + faces - 1) % faces) * tiles + tile,
    )


def halo_kernel(count, tiles, field, heads, tails, above, below, left, right, sent, got):
    bands, halo = field.shape[0], above.shape[0]
    others = sides(count, tiles)
    barrier = pltpu.get_barrier_semaphore()
    for other in others:
        pl.semaphore_signal(
            barrier, inc=1, device_id=place_of(other, tiles), device_id_type=pl.DeviceIdType.MESH
        )
    pl.semaphore_wait(barrier, 4)
    copies = []
    for i, (source, target) in enumerate((
        (field.at[pl.ds(bands - halo, halo)], above),
        (field.at[pl.ds(0, halo)], below),
        (tails, left),
        (heads, right),
    )):
        copies.append(remote(source, target, sent.at[i], got.at[i], others[i], tiles))
    tile = lax.axis_index("tile")
    first, last = tile == 0, tile == tiles - 1
    pl.when(jnp.logical_not(last))(copies[0].start)
    pl.when(jnp.logical_not(first))(copies[1].start)
    copies[2].start()
    copies[3].start()

    @pl.when(first)
    def _():
        above[...] = jnp.zeros_like(above)

    @pl.when(last)
    def _():
        below[...] = jnp.zeros_like(below)

    pl.when(jnp.logical_not(last))(copies[0].wait_send)
    pl.when(jnp.logical_not(first))(copies[0].wait_recv)
    pl.when(jnp.logical_not(first))(copies[1].wait_send)
    pl.when(jnp.logical_not(last))(copies[1].wait_recv)
    copies[2].wait()
    copies[3].wait()


def return_kernel(count, tiles, slots, returned, sent, got):
    me = lax.axis_index("face") * tiles + lax.axis_index("tile")
    greet(count, tiles, me)

    def send(s, carry):
        other = (me + s) % count
        remote(slots.at[other], returned.at[me], sent.at[s], got.at[s], other, tiles).start()
        return carry

    def wait(s, carry):
        other = (me + s) % count
        remote(slots.at[other], returned.at[me], sent.at[s], got.at[s], other, tiles).wait()
        return carry

    lax.fori_loop(1, count, send, 0)
    returned[me] = slots[me]
    lax.fori_loop(1, count, wait, 0)


def regrid_kernel(place, incoming, positions, factors, field, heads, tails, weights):
    total = factors[0] + factors[1] + factors[2] + factors[3]
    for j in range(4):
        weights[j] = factors[j] / total
    members = field.shape[1]
    lane = lax.broadcasted_iota(jnp.int32, (members, LANES), 1)
    per_tile = LANES // RANGE
    for group in range(heads.shape[0]):
        def row_step(r, carry):
            head, tail = carry
            row = group * per_tile + r
            for half in range(2):
                g = 2 * row + half
                first = incoming[place[2 * g]].astype(jnp.float32)
                second = incoming[place[2 * g + 1]].astype(jnp.float32)
                summed = None
                for j in range(4):
                    at = jnp.broadcast_to(positions[j, pl.ds(g, 1), :], (members, LANES))
                    low = at & (LANES - 1)
                    picked = jnp.where(at < LANES, lane_pick(first, low), lane_pick(second, low))
                    term = picked * weights[j, pl.ds(g, 1), :]
                    summed = term if summed is None else summed + term
                field[g] = summed
                mine = (lane >> 3) == r
                if half == 0:
                    head = jnp.where(mine, pltpu.roll(summed, r * RANGE, 1), head)
                else:
                    tail = jnp.where(mine, pltpu.roll(summed, r * RANGE + RANGE, 1), tail)
            return head, tail

        zero = jnp.zeros((members, LANES), jnp.float32)
        head, tail = lax.fori_loop(0, per_tile, row_step, (zero, zero), unroll=2)
        heads[group] = head
        tails[group] = tail


def push_of(first, second, observed_root, scale):
    diff = first - second
    square = diff * diff + FLOOR
    inverse = lax.rsqrt(square)
    root = lax.rsqrt(inverse)
    spread = jnp.sum(root, axis=0, keepdims=True) * (1.0 / first.shape[0])
    mismatch = (observed_root - spread) * scale
    return mismatch * (diff * (root * inverse * inverse))


def prepare(
    truth, heads, tails, left, right, positions, factors,
    root_tall, root_wide, root_left, root_right, high, low, tall, weights,
):
    rows = truth.shape[0]
    span = rows + RANGE
    for k in range(1, RANGE + 1):
        root = root_of(tall[pl.ds(0, span), :] - tall[pl.ds(k, span), :])
        root_tall[2 * k - 2] = root[:, :LANES]
        root_tall[2 * k - 1] = root[:, LANES:]
        west, east = truth[:, :LANES], truth[:, LANES:]
        lane = lax.broadcasted_iota(jnp.int32, west.shape, 1)
        west_next = pltpu.roll(west, LANES - k, 1)
        east_next = pltpu.roll(east, LANES - k, 1)
        root_wide[2 * k - 2] = root_of(west - jnp.where(lane < LANES - k, west_next, east_next))
        root_wide[2 * k - 1] = root_of(east - east_next)
        shift = RANGE - k
        near = heads[...]
        far = right[...]
        if shift:
            near = jnp.concatenate([near[:, LANES - shift :], near[:, : LANES - shift]], axis=1)
            far = jnp.concatenate([far[:, LANES - shift :], far[:, : LANES - shift]], axis=1)
        root_left[k - 1] = root_of(left[...] - near)
        root_right[k - 1] = root_of(tails[...] - far)
    total = factors[0] + factors[1] + factors[2] + factors[3]
    for j in range(4):
        weights[j] = factors[j] / total
    spots = lax.broadcasted_iota(jnp.int32, (2 * LANES, LANES), 0)

    def step(g, carry):
        matrix = jnp.zeros((2 * LANES, LANES), jnp.float32)
        for j in range(4):
            at = positions[j, pl.ds(g, 1), :]
            matrix = matrix + jnp.where(spots == at, weights[j, pl.ds(g, 1), :], 0.0)
        matrix = matrix.T
        top = matrix.astype(jnp.bfloat16)
        high[g] = top
        low[g] = (matrix - top.astype(jnp.float32)).astype(jnp.bfloat16)
        return carry

    lax.fori_loop(0, high.shape[0], step, 0)


def score_kernel(
    edge, place, field, above, below, heads, tails, left_tails, right_heads,
    root_tall, root_wide, root_left, root_right, high_far, low_far,
    slots, ext, grad, scales, high, low, arrived,
):
    bands, members = field.shape[0], field.shape[1]
    rows = bands // 2
    halo = 2 * RANGE
    fetch_high = pltpu.make_async_copy(high_far, high, arrived.at[0])
    fetch_low = pltpu.make_async_copy(low_far, low, arrived.at[1])
    fetch_high.start()
    fetch_low.start()
    ext[pl.ds(0, halo)] = above[...]
    ext[pl.ds(halo, bands)] = field[...]
    ext[pl.ds(halo + bands, halo)] = below[...]
    grad[...] = jnp.zeros_like(grad)

    def tall_step(a, carry):
        for half in range(2):
            mine = ext[2 * a + half]
            own = jnp.zeros_like(mine)
            for k in range(1, RANGE + 1):
                inside = (a >= edge[0]) & (a + k < edge[1])
                scale = jnp.where(inside, 1.0 / (k * members), 0.0)
                other = 2 * (a + k) + half
                push = push_of(
                    mine, ext[other],
                    root_tall[2 * k - 2 + half, pl.ds(a, 1), :], scale,
                )
                own = own - push
                grad[other] = grad[other] + push
            grad[2 * a + half] = grad[2 * a + half] + own
        return carry

    lax.fori_loop(0, rows + RANGE, tall_step, 0)

    lane = lax.broadcasted_iota(jnp.int32, (members, LANES), 1)

    sub = lane & (RANGE - 1)
    per_tile = LANES // RANGE
    for group in range(heads.shape[0]):
        head, tail = heads[group], tails[group]
        left, right = left_tails[group], right_heads[group]
        head_grad = jnp.zeros_like(head)
        tail_grad = jnp.zeros_like(tail)
        for k in range(1, RANGE + 1):
            crossing = sub >= RANGE - k
            scale = 1.0 / (k * members)
            shift = RANGE - k
            moved = pltpu.roll(head, shift, 1) if shift else head
            push = push_of(left, moved, root_left[k - 1, pl.ds(group, 1), :], scale)
            push = jnp.where(crossing, push, 0.0)
            back = pltpu.roll(push, LANES - shift, 1) if shift else push
            head_grad = head_grad + back
            moved = pltpu.roll(right, shift, 1) if shift else right
            push = push_of(tail, moved, root_right[k - 1, pl.ds(group, 1), :], scale)
            tail_grad = tail_grad - jnp.where(crossing, push, 0.0)

        def spread_step(r, carry):
            g = halo + 2 * (group * per_tile + r)
            back = pltpu.roll(head_grad, LANES - r * RANGE, 1)
            grad[g] = grad[g] + jnp.where(lane < RANGE, back, 0.0)
            back = pltpu.roll(tail_grad, LANES - RANGE - r * RANGE, 1)
            grad[g + 1] = grad[g + 1] + jnp.where(lane >= LANES - RANGE, back, 0.0)
            return carry

        lax.fori_loop(0, per_tile, spread_step, 0)

    def wide_step(r, carry):
        g = 2 * r
        west, east = field[g], field[g + 1]
        west_grad, east_grad = grad[halo + g], grad[halo + g + 1]
        for k in range(1, RANGE + 1):
            scale = 1.0 / (k * members)
            within = lane < LANES - k
            after = lane >= k
            west_next = pltpu.roll(west, LANES - k, 1)
            east_next = pltpu.roll(east, LANES - k, 1)
            west_push = push_of(
                west, jnp.where(within, west_next, east_next),
                root_wide[2 * k - 2, pl.ds(r, 1), :], scale,
            )
            east_push = push_of(
                east, east_next, root_wide[2 * k - 1, pl.ds(r, 1), :], scale
            )
            east_push = jnp.where(within, east_push, 0.0)
            west_back = pltpu.roll(west_push, k, 1)
            east_back = pltpu.roll(east_push, k, 1)
            west_grad = west_grad - west_push + jnp.where(after, west_back, 0.0)
            east_grad = east_grad - east_push + jnp.where(after, east_back, west_back)
        for half, value in ((0, west_grad), (1, east_grad)):
            adjoint(g + half, value)
        return carry

    slot_count = slots.shape[1] - 1

    def adjoint(g, value):
        value_high = value.astype(jnp.bfloat16)
        value_low = (value - value_high.astype(jnp.float32)).astype(jnp.bfloat16)
        both = jnp.concatenate([value_high, value_low], axis=0)
        main = jnp.dot(both, high[g], preferred_element_type=jnp.float32)
        slope = (
            main[:members] + main[members:]
            + jnp.dot(value_high, low[g], preferred_element_type=jnp.float32)
        )
        for half in range(2):
            part = slope[:, half * LANES : (half + 1) * LANES]
            largest = jnp.max(jnp.abs(part), axis=1, keepdims=True)
            step = jnp.maximum(largest, 1e-30) * (1.0 / STEPS)
            code = jnp.round(part * (1.0 / step)).astype(jnp.int32)
            at = place[2 * g + half]
            holder = at // slot_count
            rank = at - holder * slot_count
            slots[holder, rank] = code.astype(jnp.int16)
            power = jnp.ceil(jnp.log2(step))
            share = jnp.round(step * jnp.exp2(-power) * SHARE)
            old = scales[holder]
            old = jnp.where(lane == rank, power.astype(jnp.int32), old)
            scales[holder] = jnp.where(lane == rank + LANES // 2, share.astype(jnp.int32), old)

    fetch_high.wait()
    fetch_low.wait()
    lax.fori_loop(0, rows, wide_step, 0, unroll=2)
    for holder in range(slots.shape[0]):
        slots[holder, slot_count] = scales[holder].astype(jnp.int16)


def collect_kernel(wanted, returned, slope, summed):
    bands = slope.shape[1]
    summed[...] = jnp.zeros_like(summed)

    slot_count = returned.shape[1] - 1

    def step(d, carry):
        scale = returned[d, slot_count].astype(jnp.int32).astype(jnp.float32)
        share = pltpu.roll(scale, LANES // 2, 1) * (1.0 / SHARE)
        step_of = share * jnp.exp2(scale)
        for k in range(slot_count):
            at = wanted[d * slot_count + k]
            code = returned[d, k].astype(jnp.int32).astype(jnp.float32)
            summed[at] = summed[at] + code * step_of[:, k : k + 1]
        return carry

    lax.fori_loop(0, returned.shape[0], step, 0, unroll=4)
    for g in range(bands):
        slope[:, g, :] = summed[g]


def local(
    predicted_field,
    parent_band_holder,
    parent_band_slot,
    neighbour_positions,
    unscaled_neighbour_factor,
    truth_field,
):
    members, bands, pixels = predicted_field.shape
    tile_count = lax.axis_size("tile")
    device_count = lax.axis_size(("face", "tile"))
    slot_count = max(2, 4 * bands // device_count)
    slots_all = device_count * slot_count
    rows, cols = bands // 2, 2 * pixels
    groups = rows * RANGE // LANES

    owner = parent_band_holder.reshape(-1)
    order = jnp.arange(2 * bands, dtype=jnp.int32)
    before = (owner[:, None] == owner[None, :]) & (order[None, :] < order[:, None])
    place = owner * slot_count + jnp.sum(before.astype(jnp.int32), axis=1)
    held = place[None, :] == jnp.arange(slots_all, dtype=jnp.int32)[:, None]
    wanted = bands + jnp.sum(
        jnp.where(held, parent_band_slot.reshape(-1)[None, :] - bands, 0), axis=1
    )
    strips = jnp.transpose(predicted_field, (1, 0, 2))
    lists = jnp.pad(
        wanted.reshape(device_count, 1, slot_count), ((0, 0), (0, 0), (0, LANES - slot_count))
    )
    truth_heads = truth_field[:, :RANGE].reshape(groups, LANES)
    truth_tails = truth_field[:, cols - RANGE :].reshape(groups, LANES)
    f32 = jnp.float32
    matrices = jax.ShapeDtypeStruct((bands, pixels, 2 * pixels), jnp.bfloat16)
    incoming, asked, root_tall, root_wide, root_left, root_right, high, low = pl.pallas_call(
        functools.partial(fetch_kernel, device_count, tile_count),
        out_shape=(
            jax.ShapeDtypeStruct((device_count, slot_count, members, pixels), predicted_field.dtype),
            jax.ShapeDtypeStruct((device_count, 1, LANES), jnp.int32),
            jax.ShapeDtypeStruct((2 * RANGE, rows + RANGE, LANES), f32),
            jax.ShapeDtypeStruct((2 * RANGE, rows, LANES), f32),
            jax.ShapeDtypeStruct((RANGE, groups, LANES), f32),
            jax.ShapeDtypeStruct((RANGE, groups, LANES), f32),
            matrices,
            matrices,
        ),
        in_specs=[spec(VMEM)] * 7,
        out_specs=(spec(VMEM),) * 6 + (spec(pl.ANY),) * 2,
        scratch_shapes=[
            pltpu.VMEM((device_count, 1, LANES), jnp.int32),
            pltpu.SMEM((device_count, 1, LANES), jnp.int32),
            pltpu.VMEM((device_count, slot_count, members, pixels), predicted_field.dtype),
            pltpu.SemaphoreType.DMA((device_count,)),
            pltpu.SemaphoreType.DMA((device_count,)),
            pltpu.SemaphoreType.DMA((device_count,)),
            pltpu.SemaphoreType.DMA((device_count,)),
            pltpu.SemaphoreType.DMA,
            pltpu.VMEM((rows + 2 * RANGE, cols), f32),
            pltpu.VMEM((groups, LANES), f32),
            pltpu.VMEM((groups, LANES), f32),
            pltpu.VMEM(matrices.shape, matrices.dtype),
            pltpu.VMEM(matrices.shape, matrices.dtype),
            pltpu.VMEM((4, bands, pixels), f32),
            pltpu.SemaphoreType.DMA((4,)),
            pltpu.SemaphoreType.DMA((4,)),
            pltpu.SemaphoreType.DMA((2,)),
        ],
        compiler_params=pltpu.CompilerParams(
            collective_id=1, has_side_effects=True, vmem_limit_bytes=56 << 20
        ),
        name="fetch",
    )(
        lists, strips, truth_field, truth_heads, truth_tails,
        neighbour_positions, unscaled_neighbour_factor,
    )
    incoming = incoming.reshape(slots_all, members, pixels)
    asked = asked[:, 0, :slot_count].reshape(-1)

    side = jax.ShapeDtypeStruct((groups, members, LANES), f32)
    field, heads, tails = pl.pallas_call(
        regrid_kernel,
        out_shape=(jax.ShapeDtypeStruct((bands, members, pixels), f32), side, side),
        in_specs=[spec(SMEM), spec(VMEM), spec(VMEM), spec(VMEM)],
        out_specs=(spec(VMEM), spec(VMEM), spec(VMEM)),
        scratch_shapes=[pltpu.VMEM((4, bands, pixels), f32)],
        compiler_params=pltpu.CompilerParams(vmem_limit_bytes=56 << 20),
        name="regrid",
    )(place, incoming, neighbour_positions, unscaled_neighbour_factor)

    halo = 2 * RANGE
    strip_halo = jax.ShapeDtypeStruct((halo, members, pixels), f32)
    above, below, left_tails, right_heads = pl.pallas_call(
        functools.partial(halo_kernel, device_count, tile_count),
        out_shape=(strip_halo, strip_halo, side, side),
        in_specs=[spec(VMEM)] * 3,
        out_specs=(spec(VMEM),) * 4,
        scratch_shapes=[pltpu.SemaphoreType.DMA((4,)), pltpu.SemaphoreType.DMA((4,))],
        compiler_params=pltpu.CompilerParams(
            collective_id=2, has_side_effects=True, vmem_limit_bytes=56 << 20
        ),
        name="halo",
    )(field, heads, tails)
    tile = lax.axis_index("tile")
    edge = jnp.stack(
        [RANGE - tile * rows, RANGE + (tile_count - tile) * rows]
    ).astype(jnp.int32)

    slots = pl.pallas_call(
        score_kernel,
        out_shape=jax.ShapeDtypeStruct((device_count, slot_count + 1, members, pixels), jnp.int16),
        in_specs=[spec(SMEM), spec(SMEM)] + [spec(VMEM)] * 11 + [spec(pl.ANY)] * 2,
        out_specs=spec(VMEM),
        scratch_shapes=[
            pltpu.VMEM((bands + 2 * halo, members, pixels), f32),
            pltpu.VMEM((bands + 2 * halo, members, pixels), f32),
            pltpu.VMEM((device_count, members, pixels), jnp.int32),
            pltpu.VMEM((bands, pixels, 2 * pixels), jnp.bfloat16),
            pltpu.VMEM((bands, pixels, 2 * pixels), jnp.bfloat16),
            pltpu.SemaphoreType.DMA((2,)),
        ],
        compiler_params=pltpu.CompilerParams(vmem_limit_bytes=56 << 20),
        name="score",
    )(
        edge, place, field, above, below, heads, tails, left_tails, right_heads,
        root_tall, root_wide, root_left, root_right, high, low,
    )
    returned = pl.pallas_call(
        functools.partial(return_kernel, device_count, tile_count),
        out_shape=jax.ShapeDtypeStruct(slots.shape, slots.dtype),
        in_specs=[spec(VMEM)],
        out_specs=spec(VMEM),
        scratch_shapes=[
            pltpu.SemaphoreType.DMA((device_count,)),
            pltpu.SemaphoreType.DMA((device_count,)),
        ],
        compiler_params=pltpu.CompilerParams(
            collective_id=3, has_side_effects=True, vmem_limit_bytes=56 << 20
        ),
        name="give_back",
    )(slots)
    return pl.pallas_call(
        collect_kernel,
        out_shape=jax.ShapeDtypeStruct((members, bands, pixels), f32),
        in_specs=[spec(SMEM), spec(VMEM)],
        out_specs=spec(VMEM),
        scratch_shapes=[pltpu.VMEM((bands + 8, members, pixels), f32)],
        compiler_params=pltpu.CompilerParams(vmem_limit_bytes=56 << 20),
        name="collect",
    )(asked, returned)


def solution(mesh):
    in_specs = (
        P(None, ("face", "tile"), None),
        P(("face", "tile"), None),
        P(("face", "tile"), None),
        P(None, ("face", "tile"), None),
        P(None, ("face", "tile"), None),
        P("tile", "face"),
    )
    out_specs = P(None, ("face", "tile"), None)
    return jax.shard_map(local, mesh=mesh, in_specs=in_specs, out_specs=out_specs, check_vma=False)
```
